32 devices in a mesh: groups: 2 (over y), wide: 4 (over z), layer: 2 (over x), rep: 2 (over core).
Axes of the slice: x: 2, y: 2, z: 4, core: 2. Of those that a mesh axis runs over, the one named last changes fastest.
Arguments:
- acts: bfloat16 [48, 128, 13824], P(('groups', 'wide', 'rep'), None, 'layer'), parts along dimension 0, may hold values from -6 to 6
- grads: bfloat16 [48, 128, 5120], P(('groups', 'wide', 'rep'), None, 'layer'), parts along dimension 0, may hold values from -6 to 6
- counts: int32 [48], P(('groups', 'wide', 'rep')), parts along dimension 0, may hold values from 1 to 128, as said below
- basis_in: bfloat16 [512, 13824], P('wide', 'layer'), may hold values from -0.0546875 to 0.0546875
- basis_out: bfloat16 [512, 5120], P('wide', 'layer'), may hold values from -0.078125 to 0.078125
- query_grads: bfloat16 [64, 512, 512], P(None, ('wide', 'rep'), 'layer'), may hold values from -0.0009765625 to 0.0009765625
- eigenvalues: float32 [512, 512], P(('wide', 'rep'), 'layer'), may hold values from 0.1 to 10
- candidate: int32 [64, 2], P(('layer', 'rep'), 'groups'), parts along dimension 1, may hold values 0 or 1
Outputs:
- scores: float32 [64, 48], P(('layer', 'rep'), ('groups', 'wide')), parts along dimension 1
The draws below stay inside these ranges and needn't reach their ends.
There are 2 independent parts, one for each index of `groups`. The reference program is written for one: setup_inputs(seed, part) draws one part's arguments, and reference() takes and returns one part's arrays. A program takes and returns all parts, laid end to end along the dimension named above; an argument that names none is the same for every part. Nothing has to cross between parts.
Inputs may be any that keep to these rules, and one draw needn't show every extreme that they name: `counts`: some sequence has all 128 tokens. `candidate`: some queries are scored against a block of training sequences and some are not.
All inputs are finite; a program needn't handle non-finite values.
Results may differ from the reference program's by a relative error of at most 0.0058.
Values may be sent and summed in bfloat16 or wider, within the bound.
No kernel may reach another device: no remote copies, remote signals or barrier semaphores. Data moves between devices by JAX's collectives and lax.ppermute only.
A program may use at most 64 MiB of HBM per device.

```python
import math
import jax
import jax.numpy as jnp
from jax import lax

D = 5120
FF = 13824
KA = 512
KG = 512
LEN = 128
QUERIES = 64
SEQS = 24
BLK = 24
NBLK = 1


def draw_counts(key, part):
    key = jax.random.fold_in(key, 7)
    key_base, key_spot = jax.random.split(key)
    base = jax.random.randint(key_base, (SEQS,), 1, LEN + 1)
    spot = jax.random.randint(key_spot, (), 0, SEQS)
    return jnp.where(jnp.arange(SEQS) == spot, LEN, base).astype(jnp.int32)


def set_ends(values, stream_key, least, high):
    shape = values.shape
    index_at = [jax.random.randint(jax.random.fold_in(stream_key, axis), (), 0, shape[axis]) for axis in range(len(shape))]
    values = values.at[tuple(index_at)].set(least)
    longest = shape.index(max(shape))
    index_at[longest] = (index_at[longest] + 1) % shape[longest]
    return values.at[tuple(index_at)].set(high)


def block_scale(own_key, shape, cuts, least, largest):
    level, own = 1.0, jax.random.fold_in(own_key, 6)
    for position, parts in cuts:
        heights = jnp.exp(jax.random.uniform(jax.random.fold_in(own, position), (parts,), jnp.float32, least / len(cuts), largest / len(cuts)))
        level = level * jnp.repeat(heights, shape[position] // parts).reshape([-1 if axis == position else 1 for axis in range(len(shape))])
    return level


def bell_draw(own_key, dims, width, bound, pieces=(), kind=jnp.bfloat16):
    drawn = width * jax.random.normal(own_key, dims, jnp.float32)
    if pieces:
        drawn = drawn * block_scale(own_key, dims, pieces, -0.22, 0.18)
    return jnp.clip(drawn, -bound, bound).astype(kind)


def setup_inputs(seed: int = 0, part: int = 0) -> dict:
    arg_keys = jax.random.split(jax.random.key(seed), 9)
    part_splits = jax.random.split(jax.random.fold_in(arg_keys[8], part), 9)
    acts = bell_draw(part_splits[0], (SEQS, LEN, FF), 1.0, 6.0, ((0, 8), (2, 2)))
    grads = bell_draw(part_splits[1], (SEQS, LEN, D), 1.0, 6.0, ((0, 8), (2, 2)))
    counts = draw_counts(jax.random.fold_in(jax.random.fold_in(arg_keys[8], part), 71), part)
    basis_in = bell_draw(arg_keys[3], (KA, FF), FF ** -0.5, 0.0546875, ((0, 4), (1, 2)))
    basis_out = bell_draw(arg_keys[4], (KG, D), D ** -0.5, 0.078125, ((0, 4), (1, 2)))
    query_grads = bell_draw(arg_keys[5], (QUERIES, KG, KA), (1.0 / (4.0 * (KG * KA) ** 0.5 * (LEN / 2.0) ** 0.5)), 0.0009765625, ((1, 8), (2, 2)))
    eigenvalues = jnp.clip(jnp.exp(math.log(10.0) - 4.6051702 * jax.random.uniform(arg_keys[6], (KG, KA), jnp.float32) ** block_scale(arg_keys[6], (KG, KA), ((0, 8), (1, 2)), -0.2, 0.2)), 0.1, 10.0)
    candidate = set_ends((jax.random.randint(part_splits[7], (QUERIES, NBLK), 0, 2) < 1).astype(jnp.int32), jax.random.fold_in(part_splits[7], 1), 0, 1)
    return {"acts": acts, "grads": grads, "counts": counts, "basis_in": basis_in, "basis_out": basis_out, "query_grads": query_grads, "eigenvalues": eigenvalues, "candidate": candidate}


def one_sequence(items, basis_in, basis_out):
    tokens_in, tokens_out, alive = items
    act_rot = lax.dot_general(tokens_in, basis_in, (((1,), (1,)), ((), ())), preferred_element_type=jnp.float32).astype(jnp.bfloat16)
    grad_full = lax.dot_general(tokens_out, basis_out, (((1,), (1,)), ((), ())), preferred_element_type=jnp.float32)
    grad_rot = (grad_full * alive[:, None]).astype(jnp.bfloat16)
    return jnp.dot(grad_rot.T, act_rot, preferred_element_type=jnp.float32).astype(jnp.bfloat16)


def reference(acts, grads, counts, basis_in, basis_out, query_grads, eigenvalues, candidate):
    live = (jnp.arange(LEN, dtype=jnp.int32)[None, :] < counts[:, None]).astype(jnp.float32)
    train = lax.map(lambda items: one_sequence(items, basis_in, basis_out), (acts, grads, live))
    weighted = (query_grads.astype(jnp.float32) / eigenvalues[None, :, :]).astype(jnp.bfloat16)
    flat_query = weighted.reshape(QUERIES, KG * KA)
    flat_train = train.reshape(SEQS, KG * KA)
    raw_scores = lax.dot_general(flat_query, flat_train, (((1,), (1,)), ((), ())), preferred_element_type=jnp.float32)
    keep_mask = jnp.repeat(candidate.astype(jnp.float32), BLK, axis=1)
    return raw_scores * keep_mask
```

```python
import jax
import jax.numpy as jnp
from jax import lax
from jax.sharding import PartitionSpec as P


def swap_pairs(size, valid):
    return [(a * size + k, (1 - a) * size + k) for a in range(2) for k in range(size) if valid(k)]


def gather_rounds(own, n_wide):
    rounds = []
    held = own
    for k in range(1, n_wide):
        pairs = [(2 * w, 2 * w + 2) for w in range(k - 1, n_wide - 1)]
        pairs += [(2 * w + 3, 2 * w + 1) for w in range(0, n_wide - k)]
        held = lax.ppermute(held, ("wide", "rep"), pairs)

        def valid(place, k=k):
            w, r = divmod(place, 2)
            return w >= k if r == 0 else w <= n_wide - 1 - k

        other = lax.ppermute(held, ("groups", "wide", "rep"), swap_pairs(2 * n_wide, valid))
        across = [(p, p ^ 1) for p in range(2 * n_wide) if valid(p)]
        rounds.append(
            (
                held,
                other,
                lax.ppermute(held, ("wide", "rep"), across),
                lax.ppermute(other, ("wide", "rep"), across),
            )
        )
    return rounds


def turn(pieces, tokens):
    return lax.dot_general(
        jnp.concatenate(pieces, axis=0), tokens, (((1,), (1,)), ((), ())), preferred_element_type=jnp.float32
    )


def local(acts, grads, counts, basis_in, basis_out, query_grads, eigenvalues, candidate):
    seq_dev, seq_len, ff_local = acts.shape
    d_local = grads.shape[2]
    n_wide = lax.axis_size("wide")
    n_layer = lax.axis_size("layer")
    group, wide, layer, rep = (lax.axis_index(a) for a in ("groups", "wide", "layer", "rep"))
    n_tok = seq_dev * seq_len
    tok_in = acts.reshape(n_tok, ff_local)
    tok_out = grads.reshape(n_tok, d_local)
    rows_in, rows_out = basis_in.shape[0], basis_out.shape[0]

    def rotate(basis, tokens):
        rows = basis.shape[0]
        half = rows // 2
        own = lax.dynamic_slice_in_dim(basis, group * half, half, axis=0)
        rounds = gather_rounds(own, n_wide)
        slots = [turn([basis], tokens)]
        below, above = {}, {}
        for k, pieces in enumerate(rounds, start=1):
            y = turn(list(pieces), tokens).reshape(2, 2, half, n_tok)
            y = jnp.where(group == 0, y, y[:, ::-1]).reshape(2, rows, n_tok)
            below[k] = jnp.where(rep == 0, y[0], y[1])
            above[k] = jnp.where(rep == 0, y[1], y[0])
        for n in range(1, n_wide):
            slots.append(jnp.where(wide + n <= n_wide - 1, above[n], below[n_wide - n]))
        return jnp.stack(slots)

    grad_part = rotate(basis_out, tok_out).reshape(n_wide * rows_out, n_tok)
    act_part = rotate(basis_in, tok_in).reshape(n_wide * rows_in, n_tok)

    rank_in = n_wide * rows_in
    share = rank_in // n_layer
    doubled = jnp.concatenate([act_part, act_part], axis=0)

    def act_block(owner):
        return lax.dynamic_slice_in_dim(doubled, (owner * share - wide * rows_in) % rank_in, share, axis=0)

    grad_sum = grad_part
    act_sum = act_block(layer)
    grad_sent = grad_part.astype(jnp.bfloat16)
    for m in range(1, n_layer):
        shift = [(i, (i + m) % n_layer) for i in range(n_layer)]
        grad_sum = grad_sum + lax.ppermute(grad_sent, "layer", shift).astype(jnp.float32)
        act_sent = act_block((layer + m) % n_layer).astype(jnp.bfloat16)
        act_sum = act_sum + lax.ppermute(act_sent, "layer", shift).astype(jnp.float32)
    positions = jnp.arange(seq_len, dtype=jnp.int32)
    alive = (positions[None, :] < counts[:, None]).astype(jnp.float32).reshape(n_tok)
    grad_rot = (grad_sum * alive[None, :]).astype(jnp.bfloat16).reshape(n_wide * rows_out, seq_dev, seq_len)
    act_rot = act_sum.astype(jnp.bfloat16).reshape(share, seq_dev, seq_len)
    train = jnp.einsum("gst,ast->sga", grad_rot, act_rot, preferred_element_type=jnp.float32).astype(jnp.bfloat16)

    piece = rows_out // 2
    train = train.reshape(seq_dev, n_wide, 2, piece, share)
    mine = lax.dynamic_index_in_dim(train, rep, axis=2, keepdims=False)
    theirs = lax.ppermute(
        lax.dynamic_index_in_dim(train, 1 - rep, axis=2, keepdims=False), "rep", [(0, 1), (1, 0)]
    )
    both = jnp.stack([jnp.where(rep == 0, mine, theirs), jnp.where(rep == 0, theirs, mine)])
    both = both.reshape(2 * seq_dev, n_wide, piece, share)
    arrived = [both[:, 0]]
    for n in range(1, n_wide):
        shift = [(w, (w + n) % n_wide) for w in range(n_wide)]
        arrived.append(lax.ppermute(both[:, n], "wide", shift))
    chip_seqs = 2 * seq_dev
    train = jnp.stack(arrived).reshape(n_wide * chip_seqs, piece * share)

    n_query = query_grads.shape[0]
    weighted = (query_grads.astype(jnp.float32) / eigenvalues[None, :, :]).astype(jnp.bfloat16)
    weighted = weighted.reshape(n_query, piece * share)
    partial_value = lax.dot_general(weighted, train, (((1,), (1,)), ((), ())), preferred_element_type=jnp.float32)

    block = n_query // (2 * n_layer)
    part = partial_value.reshape(n_layer, 2, block, n_wide, chip_seqs)
    part = lax.dynamic_index_in_dim(part, rep, axis=1, keepdims=False) + lax.ppermute(
        lax.dynamic_index_in_dim(part, 1 - rep, axis=1, keepdims=False), "rep", [(0, 1), (1, 0)]
    )
    total = lax.dynamic_index_in_dim(part, layer, axis=0, keepdims=False)
    for m in range(1, n_layer):
        shift = [(i, (i + m) % n_layer) for i in range(n_layer)]
        total = total + lax.ppermute(
            lax.dynamic_index_in_dim(part, (layer + m) % n_layer, axis=0, keepdims=False), "layer", shift
        )
    scores = total[:, 0]
    for n in range(1, n_wide):
        shift = [(w, (w - n) % n_wide) for w in range(n_wide)]
        scores = scores + lax.ppermute(total[:, n], "wide", shift)

    all_seqs = n_wide * chip_seqs
    n_blocks = candidate.shape[1]
    block_size = all_seqs // n_blocks
    seq_index = wide * chip_seqs + jnp.arange(chip_seqs, dtype=jnp.int32)
    one_hot = (seq_index[None, :] // block_size == jnp.arange(n_blocks, dtype=jnp.int32)[:, None]).astype(jnp.float32)
    keep_mask = jnp.dot(candidate.astype(jnp.float32), one_hot, preferred_element_type=jnp.float32)
    return scores * keep_mask


def solution(mesh):
    in_specs = (
        P(("groups", "wide", "rep"), None, "layer"),
        P(("groups", "wide", "rep"), None, "layer"),
        P(("groups", "wide", "rep")),
        P("wide", "layer"),
        P("wide", "layer"),
        P(None, ("wide", "rep"), "layer"),
        P(("wide", "rep"), "layer"),
        P(("layer", "rep"), "groups"),
    )
    out_specs = P(("layer", "rep"), ("groups", "wide"))
    return jax.shard_map(local, mesh=mesh, in_specs=in_specs, out_specs=out_specs, check_vma=False)
```

```python
import functools

import jax
import jax.numpy as jnp
from jax import lax
from jax.experimental import pallas as pl
from jax.experimental.pallas import tpu as pltpu
from jax.sharding import PartitionSpec as P


def swap_pairs(size, valid):
    return [(a * size + k, (1 - a) * size + k) for a in range(2) for k in range(size) if valid(k)]


def gather_rounds(own, n_wide):
    rounds = []
    held = own
    for k in range(1, n_wide):
        pairs = [(2 * w, 2 * w + 2) for w in range(k - 1, n_wide - 1)]
        pairs += [(2 * w + 3, 2 * w + 1) for w in range(0, n_wide - k)]
        held = lax.ppermute(held, ("wide", "rep"), pairs)

        def valid(place, k=k):
            w, r = divmod(place, 2)
            return w >= k if r == 0 else w <= n_wide - 1 - k

        other = lax.ppermute(held, ("groups", "wide", "rep"), swap_pairs(2 * n_wide, valid))
        rounds.append((held, other))
    return rounds


def tile_of(size, most):
    return max(t for t in range(128, most + 1, 128) if size % t == 0)


def turn_body(n_pieces, *refs):
    pieces, refs = refs[:n_pieces], refs[n_pieces:]
    tokens, outs = refs[: len(refs) // 2], refs[len(refs) // 2 :]

    @pl.when(pl.program_id(0) == 0)
    def _():
        for out in outs:
            out[...] = jnp.zeros_like(out)

    panel = jnp.concatenate([p[...] for p in pieces], axis=0)
    for tok, out in zip(tokens, outs, strict=True):
        out[...] += lax.dot_general(panel, tok[...], (((1,), (1,)), ((), ())), preferred_element_type=jnp.float32)


def turn(pieces, tokens):
    rows = sum(p.shape[0] for p in pieces)
    depth = pieces[0].shape[1]
    tile = tile_of(depth, 1408)
    shapes = [jax.ShapeDtypeStruct((rows, t.shape[0]), jnp.float32) for t in tokens]
    return pl.pallas_call(
        functools.partial(turn_body, len(pieces)),
        grid=(depth // tile,),
        in_specs=[pl.BlockSpec((x.shape[0], tile), lambda k: (0, k)) for x in (*pieces, *tokens)],
        out_specs=[pl.BlockSpec(x.shape, lambda k: (0, 0)) for x in shapes],
        out_shape=shapes,
        compiler_params=pltpu.CompilerParams(vmem_limit_bytes=32 * 1024 * 1024),
        cost_estimate=pl.CostEstimate(
            flops=2 * rows * depth * sum(t.shape[0] for t in tokens),
            bytes_accessed=2 * depth * (rows + sum(t.shape[0] for t in tokens)),
            transcendentals=0,
        ),
    )(*pieces, *tokens)


def local(acts, grads, counts, basis_in, basis_out, query_grads, eigenvalues, candidate):
    seq_dev, seq_len, ff_local = acts.shape
    d_local = grads.shape[2]
    n_wide = lax.axis_size("wide")
    n_layer = lax.axis_size("layer")
    group, wide, layer, rep = (lax.axis_index(a) for a in ("groups", "wide", "layer", "rep"))
    n_tok = seq_dev * seq_len
    tok_in = acts.reshape(n_tok, ff_local)
    tok_out = grads.reshape(n_tok, d_local)
    rows_in, rows_out = basis_in.shape[0], basis_out.shape[0]

    swap = [(0, 1), (1, 0)]
    both_in = (tok_in, lax.ppermute(tok_in, "rep", swap))
    both_out = (tok_out, lax.ppermute(tok_out, "rep", swap))

    def rotate(basis, tokens):
        rows = basis.shape[0]
        half = rows // 2
        own = lax.dynamic_slice_in_dim(basis, group * half, half, axis=0)
        rounds = gather_rounds(own, n_wide)
        slots = [turn([basis], tokens[:1])[0]]
        mine, theirs = zip(*(turn(pieces, tokens) for pieces in rounds), strict=True)
        mine = jnp.stack(mine)
        theirs = lax.ppermute(jnp.stack(theirs), "rep", swap)
        sides = jnp.stack([mine, theirs]).reshape(2, n_wide - 1, 2, half, n_tok)
        sides = jnp.where(group == 0, sides, sides[:, :, ::-1]).reshape(2, n_wide - 1, rows, n_tok)
        below = jnp.where(rep == 0, sides[0], sides[1])
        above = jnp.where(rep == 0, sides[1], sides[0])
        for n in range(1, n_wide):
            slots.append(jnp.where(wide + n <= n_wide - 1, above[n - 1], below[n_wide - n - 1]))
        return jnp.stack(slots)

    grad_part = rotate(basis_out, both_out).reshape(n_wide * rows_out, n_tok)
    act_part = rotate(basis_in, both_in).reshape(n_wide * rows_in, n_tok)

    rank_in = n_wide * rows_in
    share = rank_in // n_layer
    doubled = jnp.concatenate([act_part, act_part], axis=0)

    def act_block(owner):
        return lax.dynamic_slice_in_dim(doubled, (owner * share - wide * rows_in) % rank_in, share, axis=0)

    grad_sum = grad_part
    act_sum = act_block(layer)
    grad_sent = grad_part.astype(jnp.bfloat16)
    for m in range(1, n_layer):
        shift = [(i, (i + m) % n_layer) for i in range(n_layer)]
        grad_sum = grad_sum + lax.ppermute(grad_sent, "layer", shift).astype(jnp.float32)
        act_sent = act_block((layer + m) % n_layer).astype(jnp.bfloat16)
        act_sum = act_sum + lax.ppermute(act_sent, "layer", shift).astype(jnp.float32)
    positions = jnp.arange(seq_len, dtype=jnp.int32)
    alive = (positions[None, :] < counts[:, None]).astype(jnp.float32).reshape(n_tok)
    grad_rot = (grad_sum * alive[None, :]).astype(jnp.bfloat16).reshape(n_wide * rows_out, seq_dev, seq_len)
    act_rot = act_sum.astype(jnp.bfloat16).reshape(share, seq_dev, seq_len)
    train = jnp.einsum("gst,ast->sga", grad_rot, act_rot, preferred_element_type=jnp.float32).astype(jnp.bfloat16)

    piece = rows_out // 2
    train = train.reshape(seq_dev, n_wide, 2, piece, share)
    mine = lax.dynamic_index_in_dim(train, rep, axis=2, keepdims=False)
    theirs = lax.ppermute(
        lax.dynamic_index_in_dim(train, 1 - rep, axis=2, keepdims=False), "rep", [(0, 1), (1, 0)]
    )
    both = jnp.stack([jnp.where(rep == 0, mine, theirs), jnp.where(rep == 0, theirs, mine)])
    both = both.reshape(2 * seq_dev, n_wide, piece, share)
    arrived = [both[:, 0]]
    for n in range(1, n_wide):
        shift = [(w, (w + n) % n_wide) for w in range(n_wide)]
        arrived.append(lax.ppermute(both[:, n], "wide", shift))
    chip_seqs = 2 * seq_dev
    train = jnp.stack(arrived).reshape(n_wide * chip_seqs, piece * share)

    n_query = query_grads.shape[0]
    weighted = (query_grads.astype(jnp.float32) / eigenvalues[None, :, :]).astype(jnp.bfloat16)
    weighted = weighted.reshape(n_query, piece * share)
    partial_value = lax.dot_general(weighted, train, (((1,), (1,)), ((), ())), preferred_element_type=jnp.float32)

    block = n_query // (2 * n_layer)
    part = partial_value.reshape(n_layer, 2, block, n_wide, chip_seqs)
    part = lax.dynamic_index_in_dim(part, rep, axis=1, keepdims=False) + lax.ppermute(
        lax.dynamic_index_in_dim(part, 1 - rep, axis=1, keepdims=False), "rep", [(0, 1), (1, 0)]
    )
    total = lax.dynamic_index_in_dim(part, layer, axis=0, keepdims=False)
    for m in range(1, n_layer):
        shift = [(i, (i + m) % n_layer) for i in range(n_layer)]
        total = total + lax.ppermute(
            lax.dynamic_index_in_dim(part, (layer + m) % n_layer, axis=0, keepdims=False), "layer", shift
        )
    scores = total[:, 0]
    for n in range(1, n_wide):
        shift = [(w, (w - n) % n_wide) for w in range(n_wide)]
        scores = scores + lax.ppermute(total[:, n], "wide", shift)

    all_seqs = n_wide * chip_seqs
    n_blocks = candidate.shape[1]
    block_size = all_seqs // n_blocks
    seq_index = wide * chip_seqs + jnp.arange(chip_seqs, dtype=jnp.int32)
    one_hot = (seq_index[None, :] // block_size == jnp.arange(n_blocks, dtype=jnp.int32)[:, None]).astype(jnp.float32)
    keep_mask = jnp.dot(candidate.astype(jnp.float32), one_hot, preferred_element_type=jnp.float32)
    return scores * keep_mask


def solution(mesh):
    in_specs = (
        P(("groups", "wide", "rep"), None, "layer"),
        P(("groups", "wide", "rep"), None, "layer"),
        P(("groups", "wide", "rep")),
        P("wide", "layer"),
        P("wide", "layer"),
        P(None, ("wide", "rep"), "layer"),
        P(("wide", "rep"), "layer"),
        P(("layer", "rep"), "groups"),
    )
    out_specs = P(("layer", "rep"), ("groups", "wide"))
    return jax.shard_map(local, mesh=mesh, in_specs=in_specs, out_specs=out_specs, check_vma=False)
```

```python
import functools

import jax
import jax.numpy as jnp
from jax import lax
from jax.experimental import pallas as pl
from jax.experimental.pallas import tpu as pltpu
from jax.sharding import PartitionSpec as P


def swap_pairs(size, valid):
    return [(a * size + k, (1 - a) * size + k) for a in range(2) for k in range(size) if valid(k)]


def hop_pairs(k, n_wide):
    pairs = [(2 * w, 2 * w + 2) for w in range(k - 1, n_wide - 1)]
    return pairs + [(2 * w + 3, 2 * w + 1) for w in range(0, n_wide - k)]


def holds(place, k, n_wide):
    w, r = divmod(place, 2)
    return w >= k if r == 0 else w <= n_wide - 1 - k


def gather_rounds(own, n_wide):
    rounds = []
    held = own
    for k in range(1, n_wide):
        pairs = [(2 * w, 2 * w + 2) for w in range(k - 1, n_wide - 1)]
        pairs += [(2 * w + 3, 2 * w + 1) for w in range(0, n_wide - k)]
        held = lax.ppermute(held, ("wide", "rep"), pairs)

        def valid(place, k=k):
            w, r = divmod(place, 2)
            return w >= k if r == 0 else w <= n_wide - 1 - k

        other = lax.ppermute(held, ("groups", "wide", "rep"), swap_pairs(2 * n_wide, valid))
        across = [(p, p ^ 1) for p in range(2 * n_wide) if valid(p)]
        rounds.append(
            (
                held,
                other,
                lax.ppermute(held, ("wide", "rep"), across),
                lax.ppermute(other, ("wide", "rep"), across),
            )
        )
    return rounds


def turn(pieces, tokens):
    return lax.dot_general(
        jnp.concatenate(pieces, axis=0), tokens, (((1,), (1,)), ((), ())), preferred_element_type=jnp.float32
    )


def finish(partial_value, candidate, n_wide, n_layer, chip_seqs):
    wide, layer, rep = (lax.axis_index(a) for a in ("wide", "layer", "rep"))
    n_query = partial_value.shape[0]
    block = n_query // (2 * n_layer)
    part = partial_value.reshape(n_layer, 2, block, n_wide, chip_seqs)
    part = lax.dynamic_index_in_dim(part, rep, axis=1, keepdims=False) + lax.ppermute(
        lax.dynamic_index_in_dim(part, 1 - rep, axis=1, keepdims=False), "rep", [(0, 1), (1, 0)]
    )
    total = lax.dynamic_index_in_dim(part, layer, axis=0, keepdims=False)
    for m in range(1, n_layer):
        shift = [(i, (i + m) % n_layer) for i in range(n_layer)]
        total = total + lax.ppermute(
            lax.dynamic_index_in_dim(part, (layer + m) % n_layer, axis=0, keepdims=False), "layer", shift
        )
    if n_wide & (n_wide - 1) == 0:
        doubled = jnp.concatenate([total[:, :1], total[:, :0:-1]], axis=1)
        doubled = jnp.concatenate([doubled, doubled], axis=1)
        scores = lax.dynamic_slice_in_dim(doubled, (n_wide - wide) % n_wide, n_wide, axis=1)
        bit = n_wide // 2
        while bit:
            scores = scores.reshape(block, 2, bit, chip_seqs)
            upper = (wide // bit) % 2
            keep = jnp.where(upper == 1, scores[:, 1], scores[:, 0])
            give = jnp.where(upper == 1, scores[:, 0], scores[:, 1])
            scores = keep + lax.ppermute(give, "wide", [(w, w ^ bit) for w in range(n_wide)])
            bit //= 2
        scores = scores.reshape(block, chip_seqs)
    else:
        scores = total[:, 0]
        for n in range(1, n_wide):
            shift = [(w, (w - n) % n_wide) for w in range(n_wide)]
            scores = scores + lax.ppermute(total[:, n], "wide", shift)

    all_seqs = n_wide * chip_seqs
    n_blocks = candidate.shape[1]
    block_size = all_seqs // n_blocks
    seq_index = wide * chip_seqs + jnp.arange(chip_seqs, dtype=jnp.int32)
    one_hot = (seq_index[None, :] // block_size == jnp.arange(n_blocks, dtype=jnp.int32)[:, None]).astype(jnp.float32)
    keep_mask = jnp.dot(candidate.astype(jnp.float32), one_hot, preferred_element_type=jnp.float32)
    return scores * keep_mask


def local(acts, grads, counts, basis_in, basis_out, query_grads, eigenvalues, candidate):
    seq_dev, seq_len, ff_local = acts.shape
    d_local = grads.shape[2]
    n_wide = lax.axis_size("wide")
    n_layer = lax.axis_size("layer")
    group, wide, layer, rep = (lax.axis_index(a) for a in ("groups", "wide", "layer", "rep"))
    n_tok = seq_dev * seq_len
    tok_in = acts.reshape(n_tok, ff_local)
    tok_out = grads.reshape(n_tok, d_local)
    rows_in, rows_out = basis_in.shape[0], basis_out.shape[0]

    def rotate(basis, tokens):
        rows = basis.shape[0]
        half = rows // 2
        own = lax.dynamic_slice_in_dim(basis, group * half, half, axis=0)
        rounds = gather_rounds(own, n_wide)
        slots = [turn([basis], tokens)]
        below, above = {}, {}
        for k, pieces in enumerate(rounds, start=1):
            y = turn(list(pieces), tokens).reshape(2, 2, half, n_tok)
            y = jnp.where(group == 0, y, y[:, ::-1]).reshape(2, rows, n_tok)
            below[k] = jnp.where(rep == 0, y[0], y[1])
            above[k] = jnp.where(rep == 0, y[1], y[0])
        for n in range(1, n_wide):
            slots.append(jnp.where(wide + n <= n_wide - 1, above[n], below[n_wide - n]))
        return jnp.stack(slots)

    grad_part = rotate(basis_out, tok_out).reshape(n_wide * rows_out, n_tok)
    act_part = rotate(basis_in, tok_in).reshape(n_wide * rows_in, n_tok)

    rank_in = n_wide * rows_in
    share = rank_in // n_layer
    doubled = jnp.concatenate([act_part, act_part], axis=0)

    def act_block(owner):
        return lax.dynamic_slice_in_dim(doubled, (owner * share - wide * rows_in) % rank_in, share, axis=0)

    grad_sum = grad_part
    act_sum = act_block(layer)
    grad_sent = grad_part.astype(jnp.bfloat16)
    for m in range(1, n_layer):
        shift = [(i, (i + m) % n_layer) for i in range(n_layer)]
        grad_sum = grad_sum + lax.ppermute(grad_sent, "layer", shift).astype(jnp.float32)
        act_sent = act_block((layer + m) % n_layer).astype(jnp.bfloat16)
        act_sum = act_sum + lax.ppermute(act_sent, "layer", shift).astype(jnp.float32)
    positions = jnp.arange(seq_len, dtype=jnp.int32)
    alive = (positions[None, :] < counts[:, None]).astype(jnp.float32).reshape(n_tok)
    grad_rot = (grad_sum * alive[None, :]).astype(jnp.bfloat16).reshape(n_wide * rows_out, seq_dev, seq_len)
    act_rot = act_sum.astype(jnp.bfloat16).reshape(share, seq_dev, seq_len)
    train = jnp.einsum("gst,ast->sga", grad_rot, act_rot, preferred_element_type=jnp.float32).astype(jnp.bfloat16)

    piece = rows_out // 2
    train = train.reshape(seq_dev, n_wide, 2, piece, share)
    mine = lax.dynamic_index_in_dim(train, rep, axis=2, keepdims=False)
    theirs = lax.ppermute(
        lax.dynamic_index_in_dim(train, 1 - rep, axis=2, keepdims=False), "rep", [(0, 1), (1, 0)]
    )
    both = jnp.stack([jnp.where(rep == 0, mine, theirs), jnp.where(rep == 0, theirs, mine)])
    both = both.reshape(2 * seq_dev, n_wide, piece, share)
    arrived = [both[:, 0]]
    for n in range(1, n_wide):
        shift = [(w, (w + n) % n_wide) for w in range(n_wide)]
        arrived.append(lax.ppermute(both[:, n], "wide", shift))
    chip_seqs = 2 * seq_dev
    train = jnp.stack(arrived).reshape(n_wide * chip_seqs, piece * share)

    n_query = query_grads.shape[0]
    weighted = (query_grads.astype(jnp.float32) / eigenvalues[None, :, :]).astype(jnp.bfloat16)
    weighted = weighted.reshape(n_query, piece * share)
    partial_value = lax.dot_general(weighted, train, (((1,), (1,)), ((), ())), preferred_element_type=jnp.float32)

    return finish(partial_value, candidate, n_wide, n_layer, chip_seqs)


VMEM = pl.BlockSpec(memory_space=pltpu.VMEM)
SMEM = pl.BlockSpec(memory_space=pltpu.SMEM)
ANY = pl.BlockSpec(memory_space=pl.ANY)
FLOAT, HALF = jnp.float32, jnp.bfloat16


def kernel(body, out_shape, scratch=(), flops=0, grant=6):
    return lambda **specs: pl.pallas_call(
        body,
        **specs,
        out_shape=out_shape,
        scratch_shapes=list(scratch),
        compiler_params=pltpu.CompilerParams(vmem_limit_bytes=grant * 1024 * 1024),
        cost_estimate=pl.CostEstimate(flops=flops, bytes_accessed=flops // 400 + 1024, transcendentals=0),
    )


def after(value, *earlier):
    return lax.optimization_barrier((value, *earlier))[0]


def run_copies(copies):
    for copy in copies:
        copy.start()
    for copy in copies:
        copy.wait()


def load_body(x_ref, y_ref, x_out, y_out, sems):
    run_copies(
        [pltpu.make_async_copy(x_ref, x_out, sems.at[0]), pltpu.make_async_copy(y_ref, y_out, sems.at[1])]
    )


def sum_of(blocks, start, width, tokens, t_start, total, fresh=True):
    for k in range(0, width, 1024):
        tile = min(1024, width - k)
        rows = []
        for block in blocks:
            parts = [p[:, o + start + k : o + start + k + tile] for p, o in block]
            rows.append(parts[0] if len(parts) == 1 else parts[0] + parts[1])
        part = lax.dot_general(
            tokens[:, t_start + k : t_start + k + tile],
            jnp.concatenate(rows, axis=0) if len(rows) > 1 else rows[0],
            (((1,), (1,)), ((), ())),
            preferred_element_type=FLOAT,
        )
        if fresh and k == 0:
            total[...] = part
        else:
            total[...] += part


def put(out, place, rows, value):
    out[pl.ds(pl.multiple_of(place * rows, rows), rows), :] = value


def own_body(b_out, b_in, t_out, t_in, g_own, a_own, total):
    sum_of([[(b_out, 0)]], 0, b_out.shape[1], t_out, 0, total)
    g_own[...] = total[...].T
    sum_of([[(b_in, 0)]], 0, b_in.shape[1], t_in, 0, total)
    a_own[...] = total[...].T


def first_body(at, x, y, x_far, y_far, t_out, t_in, g_first, a_first, total):
    group, rep = at[0], at[3]
    blocks = [[(p, 0)] for p in (x, y, x_far, y_far)]
    half, d = x.shape[0], t_out.shape[1]
    places = (2 * rep + group, 2 * rep + 1 - group, 2 * (1 - rep) + group, 2 * (1 - rep) + 1 - group)
    for start, tokens, out in ((0, t_out, g_first), (d, t_in, a_first)):
        sum_of(blocks, start, tokens.shape[1], tokens, 0, total)
        turned = total[...].T
        for r, place in enumerate(places):
            put(out, place, half, turned[r * half : (r + 1) * half])


def late_blocks(second, third, shift):
    x2, y2, x2_far, y2_far = second
    x3, y3, x3_far, y3_far = third
    return [
        [(x2, shift), (x2_far, shift)],
        [(y2, shift), (y2_far, shift)],
        [(x3, 0), (x3_far, 0)],
        [(y3, 0), (y3_far, 0)],
    ]


def place_all(at, own, first, total, store):
    group, wide = at[0], at[1]
    rows = own.shape[0]
    half = rows // 2
    store(0, own[...], None)
    store(1, first[rows:, :], wide <= 2)
    store(3, first[:rows, :], wide >= 1)
    turned = total[...].T

    def ordered(k):
        mine, other = (turned[(2 * k + i) * half : (2 * k + i + 1) * half] for i in range(2))
        return jnp.concatenate(
            [jnp.where(group == 0, mine, other), jnp.where(group == 0, other, mine)], axis=0
        )

    store(2, ordered(0), None)
    last = ordered(1)
    store(1, last, wide == 3)
    store(3, last, wide == 0)


def when(condition, do):
    if condition is None:
        do()
    else:
        pl.when(condition)(do)


def out_body(n_second, at, *refs):
    second, third = refs[:4], refs[4:8]
    t_out, t_in, own, first, grad, grad_sent, part, total = refs[8:]
    blocks = late_blocks(second, third, 0)
    d = t_out.shape[1]
    sum_of(blocks, 0, d, t_out, 0, total)

    def store(slot, value, condition):
        rows = value.shape[0]

        def do():
            grad[slot * rows : (slot + 1) * rows, :] = value
            grad_sent[slot * rows : (slot + 1) * rows, :] = value.astype(HALF)

        when(condition, do)

    place_all(at, own, first, total, store)
    sum_of(blocks, d, third[0].shape[1] - d, t_in, 0, part)


def in_body(shift, at, *refs):
    second, third = refs[:4], refs[4:8]
    t_in, part, own, first, mine, sent, total = refs[8:]
    total[...] = part[...]
    width = third[0].shape[1]
    sum_of(late_blocks(second, third, shift), 0, width, t_in, t_in.shape[1] - width, total, fresh=False)
    wide, layer = at[1], at[2]

    def store(slot, value, condition):
        rows = value.shape[0]
        shard = lax.rem(wide + slot, 4)
        per_layer = mine.shape[0] // rows
        place = lax.rem(shard, per_layer)
        here = lax.div(shard, per_layer) == layer

        def keep():
            put(mine, place, rows, value)

        def send():
            put(sent, place, rows, value.astype(HALF))

        both = (here, jnp.logical_not(here)) if condition is None else (condition & here, condition & jnp.logical_not(here))
        pl.when(both[0])(keep)
        pl.when(both[1])(send)

    place_all(at, own, first, total, store)


def train_body(at, counts, grad, grad_came, act, act_came, *refs):
    mine, theirs, held = refs[:4], refs[4:8], refs[8]
    rep = at[3]
    seqs, half = mine[0].shape[0], mine[0].shape[1]
    length = grad.shape[1] // seqs
    spot = lax.broadcasted_iota(jnp.int32, (1, length), 1)
    for s in range(seqs):
        cols = slice(s * length, (s + 1) * length)
        g = grad[:, cols] + grad_came[:, cols].astype(FLOAT)
        g = jnp.where(spot < counts[s], g, 0.0).astype(HALF)
        a = (act[:, cols] + act_came[:, cols].astype(FLOAT)).astype(HALF)
        held[...] = lax.dot_general(g, a, (((1,), (1,)), ((), ())), preferred_element_type=FLOAT).astype(HALF)
        for n in range(4):
            for r, outs in ((rep, mine), (1 - rep, theirs)):
                outs[n][s] = held[pl.ds(pl.multiple_of((2 * n + r) * half, half), half), :]


def shaped(*shape, kind=FLOAT):
    return jax.ShapeDtypeStruct(shape, kind)


def local_fast(acts, grads, counts, basis_in, basis_out, query_grads, eigenvalues, candidate):
    n_wide, n_layer = 4, 2
    seq_dev, seq_len, ff = acts.shape
    d = grads.shape[2]
    n_tok = seq_dev * seq_len
    rows = basis_in.shape[0]
    half = rows // 2
    share = n_wide * rows // n_layer
    group, wide, layer, rep = (lax.axis_index(a) for a in ("groups", "wide", "layer", "rep"))
    at = jnp.stack([group, wide, layer, rep]).astype(jnp.int32)
    swap = [(0, 1), (1, 0)]
    dma = pltpu.SemaphoreType.DMA((2,))

    held = jnp.concatenate(
        [lax.dynamic_slice_in_dim(x, group * half, half, axis=0) for x in (basis_out, basis_in)], axis=1
    )
    t_out, t_in = kernel(
        load_body, [pltpu.VMEM((n_tok, d), HALF), pltpu.VMEM((n_tok, ff), HALF)], [dma], grant=4
    )(in_specs=[ANY, ANY], out_specs=[VMEM, VMEM])(grads.reshape(n_tok, d), acts.reshape(n_tok, ff))
    g_own, a_own = kernel(
        own_body, [shaped(rows, n_tok)] * 2, [pltpu.VMEM((n_tok, rows), FLOAT)], 2 * rows * n_tok * (d + ff)
    )(in_specs=[VMEM] * 4, out_specs=[VMEM] * 2)(basis_out, basis_in, t_out, t_in)

    def to_group(x, k):
        pairs = swap_pairs(2 * n_wide, functools.partial(holds, k=k, n_wide=n_wide))
        return lax.ppermute(x, ("groups", "wide", "rep"), pairs)

    def to_core(x, k):
        return lax.ppermute(x, ("wide", "rep"), [(p, p ^ 1) for p in range(2 * n_wide) if holds(p, k, n_wide)])

    def hop(x, k):
        return lax.ppermute(x, ("wide", "rep"), hop_pairs(k, n_wide))

    x1 = hop(held, 1)
    y1 = to_group(x1, 1)
    x2 = hop(after(x1, g_own, a_own), 2)
    y2 = to_group(x2, 2)
    cut = (ff - d) // 256 * 128
    x3 = [hop(x2[:, : d + cut], 3), hop(x2[:, d + cut :], 3)]
    y3 = [to_group(x, 3) for x in x3]

    def on_both(x, y, k, *earlier):
        return x, y, to_core(after(x, *earlier), k), to_core(after(y, *earlier), k)

    first = on_both(x1, y1, 1, *x3)
    g_first, a_first = kernel(
        first_body, [shaped(2 * rows, n_tok)] * 2, [pltpu.VMEM((n_tok, 2 * rows), FLOAT)], 4 * rows * n_tok * (d + ff)
    )(in_specs=[SMEM] + [VMEM] * 6, out_specs=[VMEM] * 2)(at, *first, t_out, t_in)
    second = on_both(x2, y2, 2, *x3)
    thirds = [on_both(x3[0], y3[0], 3), on_both(x3[1], y3[1], 3)]

    wide_sum = pltpu.VMEM((n_tok, 2 * rows), FLOAT)
    grad, grad_sent, part = kernel(
        functools.partial(out_body, 4),
        [shaped(n_wide * rows, n_tok), shaped(n_wide * rows, n_tok, kind=HALF), shaped(n_tok, 2 * rows)],
        [wide_sum],
        4 * rows * n_tok * (d + cut),
    )(in_specs=[SMEM] + [VMEM] * 12, out_specs=[VMEM] * 3)(
        at, *second, *thirds[0], t_out, t_in, g_own, g_first
    )
    grad_came = lax.ppermute(grad_sent, "layer", swap)
    act, act_sent = kernel(
        functools.partial(in_body, d + cut),
        [shaped(share, n_tok), shaped(share, n_tok, kind=HALF)],
        [wide_sum],
        4 * rows * n_tok * (ff - cut),
    )(in_specs=[SMEM] + [VMEM] * 12, out_specs=[VMEM] * 2)(
        at, *second, *thirds[1], t_in, part, a_own, a_first
    )
    act_came = lax.ppermute(after(act_sent, grad_came), "layer", swap)

    pieces = kernel(
        train_body,
        [shaped(seq_dev, half, share, kind=HALF)] * 8,
        [pltpu.VMEM((n_wide * rows, share), HALF)],
        2 * n_wide * rows * share * n_tok,
    )(in_specs=[SMEM, SMEM] + [VMEM] * 4, out_specs=[VMEM] * 8)(at, counts, grad, grad_came, act, act_came)
    mine, theirs = pieces[:4], pieces[4:]

    def send(x, n, cross):
        pairs = [(2 * w + r, 2 * ((w + n) % n_wide) + (r ^ cross)) for w in range(n_wide) for r in range(2)]
        return lax.ppermute(x, ("wide", "rep"), pairs)

    same = [mine[0]] + [send(mine[n], n, 0) for n in range(1, n_wide)]
    cross = [send(theirs[n], n, 1) for n in range(n_wide)]
    chip_seqs = 2 * seq_dev
    train = jnp.stack([jnp.stack([a, b]) for a, b in zip(same, cross, strict=True)])
    train = train.reshape(n_wide * chip_seqs, half * share)
    n_query = query_grads.shape[0]
    weighted = (query_grads.astype(FLOAT) / eigenvalues[None, :, :]).astype(HALF).reshape(n_query, half * share)
    scored = lax.dot_general(weighted, train, (((1,), (1,)), ((), ())), preferred_element_type=FLOAT)
    scored = scored.reshape(n_query, n_wide, 2, seq_dev)
    scored = jnp.where(rep == 0, scored, scored[:, :, ::-1]).reshape(n_query, n_wide * chip_seqs)
    return finish(scored, candidate, n_wide, n_layer, chip_seqs)


def solution(mesh):
    sizes = tuple(mesh.shape[a] for a in ("groups", "wide", "layer", "rep"))
    body = local_fast if sizes == (2, 4, 2, 2) else local
    in_specs = (
        P(("groups", "wide", "rep"), None, "layer"),
        P(("groups", "wide", "rep"), None, "layer"),
        P(("groups", "wide", "rep")),
        P("wide", "layer"),
        P("wide", "layer"),
        P(None, ("wide", "rep"), "layer"),
        P(("wide", "rep"), "layer"),
        P(("layer", "rep"), "groups"),
    )
    out_specs = P(("layer", "rep"), ("groups", "wide"))
    return jax.shard_map(body, mesh=mesh, in_specs=in_specs, out_specs=out_specs, check_vma=False)
```

```python
import functools

import jax
import jax.numpy as jnp
from jax import lax
from jax.experimental import pallas as pl
from jax.experimental.pallas import tpu as pltpu
from jax.sharding import PartitionSpec as P


def swap_pairs(size, valid):
    return [(a * size + k, (1 - a) * size + k) for a in range(2) for k in range(size) if valid(k)]


def hop_pairs(k, n_wide):
    pairs = [(2 * w, 2 * w + 2) for w in range(k - 1, n_wide - 1)]
    return pairs + [(2 * w + 3, 2 * w + 1) for w in range(0, n_wide - k)]


def gather_rounds(own, n_wide):
    rounds = []
    held = own
    for k in range(1, n_wide):
        pairs = [(2 * w, 2 * w + 2) for w in range(k - 1, n_wide - 1)]
        pairs += [(2 * w + 3, 2 * w + 1) for w in range(0, n_wide - k)]
        held = lax.ppermute(held, ("wide", "rep"), pairs)

        def valid(place, k=k):
            w, r = divmod(place, 2)
            return w >= k if r == 0 else w <= n_wide - 1 - k

        other = lax.ppermute(held, ("groups", "wide", "rep"), swap_pairs(2 * n_wide, valid))
        across = [(p, p ^ 1) for p in range(2 * n_wide) if valid(p)]
        rounds.append(
            (
                held,
                other,
                lax.ppermute(held, ("wide", "rep"), across),
                lax.ppermute(other, ("wide", "rep"), across),
            )
        )
    return rounds


def turn(pieces, tokens):
    return lax.dot_general(
        jnp.concatenate(pieces, axis=0), tokens, (((1,), (1,)), ((), ())), preferred_element_type=jnp.float32
    )


def finish(partial_value, candidate, n_wide, n_layer, chip_seqs):
    wide, layer, rep = (lax.axis_index(a) for a in ("wide", "layer", "rep"))
    n_query = partial_value.shape[0]
    block = n_query // (2 * n_layer)
    part = partial_value.reshape(n_layer, 2, block, n_wide, chip_seqs)
    part = lax.dynamic_index_in_dim(part, rep, axis=1, keepdims=False) + lax.ppermute(
        lax.dynamic_index_in_dim(part, 1 - rep, axis=1, keepdims=False), "rep", [(0, 1), (1, 0)]
    )
    total = lax.dynamic_index_in_dim(part, layer, axis=0, keepdims=False)
    for m in range(1, n_layer):
        shift = [(i, (i + m) % n_layer) for i in range(n_layer)]
        total = total + lax.ppermute(
            lax.dynamic_index_in_dim(part, (layer + m) % n_layer, axis=0, keepdims=False), "layer", shift
        )
    if n_wide & (n_wide - 1) == 0:
        doubled = jnp.concatenate([total[:, :1], total[:, :0:-1]], axis=1)
        doubled = jnp.concatenate([doubled, doubled], axis=1)
        scores = lax.dynamic_slice_in_dim(doubled, (n_wide - wide) % n_wide, n_wide, axis=1)
        bit = n_wide // 2
        while bit:
            scores = scores.reshape(block, 2, bit, chip_seqs)
            upper = (wide // bit) % 2
            keep = jnp.where(upper == 1, scores[:, 1], scores[:, 0])
            give = jnp.where(upper == 1, scores[:, 0], scores[:, 1])
            scores = keep + lax.ppermute(give, "wide", [(w, w ^ bit) for w in range(n_wide)])
            bit //= 2
        scores = scores.reshape(block, chip_seqs)
    else:
        scores = total[:, 0]
        for n in range(1, n_wide):
            shift = [(w, (w - n) % n_wide) for w in range(n_wide)]
            scores = scores + lax.ppermute(total[:, n], "wide", shift)

    all_seqs = n_wide * chip_seqs
    n_blocks = candidate.shape[1]
    block_size = all_seqs // n_blocks
    seq_index = wide * chip_seqs + jnp.arange(chip_seqs, dtype=jnp.int32)
    one_hot = (seq_index[None, :] // block_size == jnp.arange(n_blocks, dtype=jnp.int32)[:, None]).astype(jnp.float32)
    keep_mask = jnp.dot(candidate.astype(jnp.float32), one_hot, preferred_element_type=jnp.float32)
    return scores * keep_mask


def local(acts, grads, counts, basis_in, basis_out, query_grads, eigenvalues, candidate):
    seq_dev, seq_len, ff_local = acts.shape
    d_local = grads.shape[2]
    n_wide = lax.axis_size("wide")
    n_layer = lax.axis_size("layer")
    group, wide, layer, rep = (lax.axis_index(a) for a in ("groups", "wide", "layer", "rep"))
    n_tok = seq_dev * seq_len
    tok_in = acts.reshape(n_tok, ff_local)
    tok_out = grads.reshape(n_tok, d_local)
    rows_in, rows_out = basis_in.shape[0], basis_out.shape[0]

    def rotate(basis, tokens):
        rows = basis.shape[0]
        half = rows // 2
        own = lax.dynamic_slice_in_dim(basis, group * half, half, axis=0)
        rounds = gather_rounds(own, n_wide)
        slots = [turn([basis], tokens)]
        below, above = {}, {}
        for k, pieces in enumerate(rounds, start=1):
            y = turn(list(pieces), tokens).reshape(2, 2, half, n_tok)
            y = jnp.where(group == 0, y, y[:, ::-1]).reshape(2, rows, n_tok)
            below[k] = jnp.where(rep == 0, y[0], y[1])
            above[k] = jnp.where(rep == 0, y[1], y[0])
        for n in range(1, n_wide):
            slots.append(jnp.where(wide + n <= n_wide - 1, above[n], below[n_wide - n]))
        return jnp.stack(slots)

    grad_part = rotate(basis_out, tok_out).reshape(n_wide * rows_out, n_tok)
    act_part = rotate(basis_in, tok_in).reshape(n_wide * rows_in, n_tok)

    rank_in = n_wide * rows_in
    share = rank_in // n_layer
    doubled = jnp.concatenate([act_part, act_part], axis=0)

    def act_block(owner):
        return lax.dynamic_slice_in_dim(doubled, (owner * share - wide * rows_in) % rank_in, share, axis=0)

    grad_sum = grad_part
    act_sum = act_block(layer)
    grad_sent = grad_part.astype(jnp.bfloat16)
    for m in range(1, n_layer):
        shift = [(i, (i + m) % n_layer) for i in range(n_layer)]
        grad_sum = grad_sum + lax.ppermute(grad_sent, "layer", shift).astype(jnp.float32)
        act_sent = act_block((layer + m) % n_layer).astype(jnp.bfloat16)
        act_sum = act_sum + lax.ppermute(act_sent, "layer", shift).astype(jnp.float32)
    positions = jnp.arange(seq_len, dtype=jnp.int32)
    alive = (positions[None, :] < counts[:, None]).astype(jnp.float32).reshape(n_tok)
    grad_rot = (grad_sum * alive[None, :]).astype(jnp.bfloat16).reshape(n_wide * rows_out, seq_dev, seq_len)
    act_rot = act_sum.astype(jnp.bfloat16).reshape(share, seq_dev, seq_len)
    train = jnp.einsum("gst,ast->sga", grad_rot, act_rot, preferred_element_type=jnp.float32).astype(jnp.bfloat16)

    piece = rows_out // 2
    train = train.reshape(seq_dev, n_wide, 2, piece, share)
    mine = lax.dynamic_index_in_dim(train, rep, axis=2, keepdims=False)
    theirs = lax.ppermute(
        lax.dynamic_index_in_dim(train, 1 - rep, axis=2, keepdims=False), "rep", [(0, 1), (1, 0)]
    )
    both = jnp.stack([jnp.where(rep == 0, mine, theirs), jnp.where(rep == 0, theirs, mine)])
    both = both.reshape(2 * seq_dev, n_wide, piece, share)
    arrived = [both[:, 0]]
    for n in range(1, n_wide):
        shift = [(w, (w + n) % n_wide) for w in range(n_wide)]
        arrived.append(lax.ppermute(both[:, n], "wide", shift))
    chip_seqs = 2 * seq_dev
    train = jnp.stack(arrived).reshape(n_wide * chip_seqs, piece * share)

    n_query = query_grads.shape[0]
    weighted = (query_grads.astype(jnp.float32) / eigenvalues[None, :, :]).astype(jnp.bfloat16)
    weighted = weighted.reshape(n_query, piece * share)
    partial_value = lax.dot_general(weighted, train, (((1,), (1,)), ((), ())), preferred_element_type=jnp.float32)

    return finish(partial_value, candidate, n_wide, n_layer, chip_seqs)


VMEM = pl.BlockSpec(memory_space=pltpu.VMEM)
SMEM = pl.BlockSpec(memory_space=pltpu.SMEM)
ANY = pl.BlockSpec(memory_space=pl.ANY)
FLOAT, HALF = jnp.float32, jnp.bfloat16


def kernel(body, out_shape, scratch=(), flops=0, grant=12):
    return lambda **specs: pl.pallas_call(
        body,
        **specs,
        out_shape=out_shape,
        scratch_shapes=list(scratch),
        compiler_params=pltpu.CompilerParams(vmem_limit_bytes=grant * 1024 * 1024),
        cost_estimate=pl.CostEstimate(flops=flops // 1000, bytes_accessed=1024, transcendentals=0),
    )


def after(value, *earlier):
    return lax.optimization_barrier((value, *earlier))[0]


def run_copies(copies):
    for copy in copies:
        copy.start()
    for copy in copies:
        copy.wait()


def load_body(x_ref, y_ref, x_out, y_out, sems):
    run_copies(
        [pltpu.make_async_copy(x_ref, x_out, sems.at[0]), pltpu.make_async_copy(y_ref, y_out, sems.at[1])]
    )


def sum_of(pieces, start, width, tokens, t_start, total, fresh=True):
    for k in range(0, width, 1024):
        tile = min(1024, width - k)
        rows = [p[:, start + k : start + k + tile] for p in pieces]
        part = lax.dot_general(
            tokens[:, t_start + k : t_start + k + tile],
            jnp.concatenate(rows, axis=0) if len(rows) > 1 else rows[0],
            (((1,), (1,)), ((), ())),
            preferred_element_type=FLOAT,
        )
        if fresh and k == 0:
            total[...] = part
        else:
            total[...] += part


def put(out, place, rows, value):
    out[pl.ds(pl.multiple_of(place * rows, rows), rows), :] = value


def own_body(b_out, b_in, t_out, t_in, g_own, a_own, total):
    sum_of([b_out], 0, b_out.shape[1], t_out, 0, total)
    g_own[...] = total[...].T
    sum_of([b_in], 0, b_in.shape[1], t_in, 0, total)
    a_own[...] = total[...].T


def in_order(group, turned):
    half = turned.shape[0] // 2
    mine, other = turned[:half], turned[half:]
    return jnp.concatenate([jnp.where(group == 0, mine, other), jnp.where(group == 0, other, mine)], axis=0)


def shard_body(flag, at, x, y, t_out, t_in, o_out, o_in, mine, theirs, held, total, sems):
    d, ff = t_out.shape[1], t_in.shape[1]
    rows = mine.shape[0] // 2
    cuts = [(0, d)] + [(d + k, min(ff // 2 // 128 * 128 + 128, ff - k)) for k in range(0, ff, ff // 2 // 128 * 128 + 128)]
    cuts = [(start, width) for start, width in cuts if width > 0]

    @pl.when(at[flag] == 1)
    def _():
        copies = []
        for i, (start, width) in enumerate(cuts):
            columns = pl.ds(start, width)
            copies.append(
                [
                    pltpu.make_async_copy(p.at[:, columns], held.at[j, :, columns], sems.at[i, j])
                    for j, p in enumerate((x, y))
                ]
            )
        for pair in copies:
            for copy in pair:
                copy.start()
        for i, (start, width) in enumerate(cuts):
            for copy in copies[i]:
                copy.wait()
            for j, tokens in enumerate((t_out, o_out) if start < d else (t_in, o_in)):
                first = start if start < d else start - d
                sum_of([held.at[0], held.at[1]], start, width, tokens, first, total.at[j], first == 0)
            if i == 0 or i == len(cuts) - 1:
                put_rows = slice(0, rows) if i == 0 else slice(rows, 2 * rows)
                for j, out in enumerate((mine, theirs)):
                    out[put_rows, :] = in_order(at[0], total[j].T)


def when(condition, do):
    if condition is None:
        do()
    else:
        pl.when(condition)(do)


def slots_body(at, g_own, a_own, near, near_far, middle, middle_far, inner, inner_far, outer, outer_far, *outs):
    grad, grad_sent, act, act_sent = outs
    wide, layer, holds = at[1], at[2], at[4] == 1
    rows = g_own.shape[0]

    def store(slot, value, condition, is_out):
        if is_out:

            def do():
                grad[slot * rows : (slot + 1) * rows, :] = value()
                grad_sent[slot * rows : (slot + 1) * rows, :] = value().astype(HALF)

            when(condition, do)
            return
        shard = lax.rem(wide + slot, 4)
        per_layer = act.shape[0] // rows
        place = lax.rem(shard, per_layer)
        here = lax.div(shard, per_layer) == layer
        away = jnp.logical_not(here)
        pl.when(here if condition is None else condition & here)(lambda: put(act, place, rows, value()))
        pl.when(away if condition is None else condition & away)(
            lambda: put(act_sent, place, rows, value().astype(HALF))
        )

    for is_out in (True, False):
        part = slice(0, rows) if is_out else slice(rows, 2 * rows)
        other = jnp.logical_not(holds)
        own = g_own if is_out else a_own
        store(0, lambda own=own: own[...], None, is_out)
        for slot, here, away, condition, at_holder in (
            (1, near, near_far, wide <= 1, holds),
            (3, near, near_far, wide >= 2, holds),
            (2, middle, middle_far, None, holds),
            (3, inner, inner_far, wide == 1, other),
            (1, inner, inner_far, wide == 2, other),
            (3, outer, outer_far, wide == 0, holds),
            (1, outer, outer_far, wide == 3, holds),
        ):
            for source, at_this in ((here, at_holder), (away, jnp.logical_not(at_holder))):
                both = at_this if condition is None else condition & at_this
                store(slot, lambda source=source, part=part: source[part, :], both, is_out)


def train_body(at, counts, grad, grad_came, act, act_came, *refs):
    mine, theirs, held = refs[:4], refs[4:8], refs[8]
    rep = at[3]
    seqs, half = mine[0].shape[0], mine[0].shape[1]
    length = grad.shape[1] // seqs
    spot = lax.broadcasted_iota(jnp.int32, (1, length), 1)
    for s in range(seqs):
        cols = slice(s * length, (s + 1) * length)
        g = grad[:, cols] + grad_came[:, cols].astype(FLOAT)
        g = jnp.where(spot < counts[s], g, 0.0).astype(HALF)
        a = (act[:, cols] + act_came[:, cols].astype(FLOAT)).astype(HALF)
        held[...] = lax.dot_general(g, a, (((1,), (1,)), ((), ())), preferred_element_type=FLOAT).astype(HALF)
        for n in range(4):
            for r, outs in ((rep, mine), (1 - rep, theirs)):
                outs[n][s] = held[pl.ds(pl.multiple_of((2 * n + r) * half, half), half), :]


def shaped(*shape, kind=FLOAT):
    return jax.ShapeDtypeStruct(shape, kind)


def local_fast(acts, grads, counts, basis_in, basis_out, query_grads, eigenvalues, candidate):
    n_wide, n_layer = 4, 2
    seq_dev, seq_len, ff = acts.shape
    d = grads.shape[2]
    n_tok = seq_dev * seq_len
    rows = basis_in.shape[0]
    half = rows // 2
    share = n_wide * rows // n_layer
    group, wide, layer, rep = (lax.axis_index(a) for a in ("groups", "wide", "layer", "rep"))
    holds = (rep == 1) == (wide <= 1)
    outside = (wide == 0) | (wide == 3)
    at = jnp.stack([group, wide, layer, rep, holds, ~holds & ~outside, holds & outside]).astype(jnp.int32)
    swap = [(0, 1), (1, 0)]
    n_query = query_grads.shape[0]
    weighted = (query_grads.astype(FLOAT) / eigenvalues[None, :, :]).astype(HALF).reshape(n_query, half * share)
    dma = pltpu.SemaphoreType.DMA((2,))

    held = jnp.concatenate(
        [lax.dynamic_slice_in_dim(x, group * half, half, axis=0) for x in (basis_out, basis_in)], axis=1
    )

    def load(x, y):
        return kernel(
            load_body, [pltpu.VMEM((n_tok, d), HALF), pltpu.VMEM((n_tok, ff), HALF)], [dma], grant=4
        )(in_specs=[ANY, ANY], out_specs=[VMEM, VMEM])(x.reshape(n_tok, d), y.reshape(n_tok, ff))

    t_out, t_in = load(grads, acts)
    g_own, a_own = kernel(
        own_body, [shaped(rows, n_tok)] * 2, [pltpu.VMEM((n_tok, rows), FLOAT)], 2 * rows * n_tok * (d + ff)
    )(in_specs=[VMEM] * 4, out_specs=[VMEM] * 2)(basis_out, basis_in, t_out, t_in)

    near = [(0, 1), (1, 1), (2, 0), (3, 0)]
    inner = [(1, 0), (2, 1)]
    outer = [(0, 1), (3, 0)]

    def to_group(x, places):
        numbers = {2 * w + r for w, r in places}
        return lax.ppermute(x, ("groups", "wide", "rep"), swap_pairs(2 * n_wide, numbers.__contains__))

    def hop(x, k):
        return lax.ppermute(x, ("wide", "rep"), hop_pairs(k, n_wide))

    o_out, o_in = load(lax.ppermute(grads, "rep", swap), lax.ppermute(acts, "rep", swap))

    def rotate(flag, x, y):
        both = 2 * rows
        mine, theirs = kernel(
            functools.partial(shard_body, flag),
            [shaped(both, n_tok)] * 2,
            [pltpu.VMEM((2, half, d + ff), HALF), pltpu.VMEM((2, n_tok, rows), FLOAT), pltpu.SemaphoreType.DMA((4, 2))],
            4 * rows * n_tok * (d + ff),
        )(in_specs=[SMEM, ANY, ANY] + [VMEM] * 4, out_specs=[VMEM] * 2)(at, x, y, t_out, t_in, o_out, o_in)
        return mine, lax.ppermute(theirs, "rep", swap)

    x1 = hop(held, 1)
    y1 = to_group(x1, near)
    x1_sent, weighted, _, _ = lax.optimization_barrier((x1, weighted, g_own, a_own))
    x2 = hop(x1_sent, 2)
    x3 = hop(after(x2, y1), 3)
    y2 = to_group(x2, near)
    near_done = rotate(4, x1, y1)
    y3 = to_group(after(x3, y2, near_done[0]), outer)
    y1_inner = to_group(after(x1, y1), inner)
    middle_done = rotate(4, x2, y2)
    inner_done = rotate(5, x1, y1_inner)
    outer_done = rotate(6, x3, after(y3, middle_done[0], inner_done[0]))

    all_rows = n_wide * rows
    grad, grad_sent, act, act_sent = kernel(
        slots_body,
        [shaped(r, n_tok, kind=kind) for r in (all_rows, share) for kind in (FLOAT, HALF)],
    )(in_specs=[SMEM] + [VMEM] * 10, out_specs=[VMEM] * 4)(
        at, g_own, a_own, *near_done, *middle_done, *inner_done, *outer_done
    )
    grad_came = lax.ppermute(grad_sent, "layer", swap)
    act_came = lax.ppermute(act_sent, "layer", swap)

    pieces = kernel(
        train_body,
        [shaped(seq_dev, half, share, kind=HALF)] * 8,
        [pltpu.VMEM((n_wide * rows, share), HALF)],
        2 * n_wide * rows * share * n_tok,
    )(in_specs=[SMEM, SMEM] + [VMEM] * 4, out_specs=[VMEM] * 8)(at, counts, grad, grad_came, act, act_came)
    mine, theirs = pieces[:4], pieces[4:]

    def send(x, n, cross):
        pairs = [(2 * w + r, 2 * ((w + n) % n_wide) + (r ^ cross)) for w in range(n_wide) for r in range(2)]
        return lax.ppermute(x, ("wide", "rep"), pairs)

    same = [mine[0]] + [send(mine[n], n, 0) for n in range(1, n_wide)]
    cross = [send(theirs[n], n, 1) for n in range(n_wide)]
    chip_seqs = 2 * seq_dev
    train = jnp.stack([jnp.stack([a, b]) for a, b in zip(same, cross, strict=True)])
    train = train.reshape(n_wide * chip_seqs, half * share)
    scored = lax.dot_general(weighted, train, (((1,), (1,)), ((), ())), preferred_element_type=FLOAT)
    scored = scored.reshape(n_query, n_wide, 2, seq_dev)
    scored = jnp.where(rep == 0, scored, scored[:, :, ::-1]).reshape(n_query, n_wide * chip_seqs)
    return finish(scored, candidate, n_wide, n_layer, chip_seqs)


def solution(mesh):
    sizes = tuple(mesh.shape[a] for a in ("groups", "wide", "layer", "rep"))
    body = local_fast if sizes == (2, 4, 2, 2) else local
    in_specs = (
        P(("groups", "wide", "rep"), None, "layer"),
        P(("groups", "wide", "rep"), None, "layer"),
        P(("groups", "wide", "rep")),
        P("wide", "layer"),
        P("wide", "layer"),
        P(None, ("wide", "rep"), "layer"),
        P(("wide", "rep"), "layer"),
        P(("layer", "rep"), "groups"),
    )
    out_specs = P(("layer", "rep"), ("groups", "wide"))
    return jax.shard_map(body, mesh=mesh, in_specs=in_specs, out_specs=out_specs, check_vma=False)
```

```python
import functools

import jax
import jax.numpy as jnp
from jax import lax
from jax.experimental import pallas as pl
from jax.experimental.pallas import tpu as pltpu
from jax.sharding import PartitionSpec as P


def swap_pairs(size, valid):
    return [(a * size + k, (1 - a) * size + k) for a in range(2) for k in range(size) if valid(k)]


def hop_pairs(k, n_wide):
    pairs = [(2 * w, 2 * w + 2) for w in range(k - 1, n_wide - 1)]
    return pairs + [(2 * w + 3, 2 * w + 1) for w in range(0, n_wide - k)]


def gather_rounds(own, n_wide):
    rounds = []
    held = own
    for k in range(1, n_wide):
        pairs = [(2 * w, 2 * w + 2) for w in range(k - 1, n_wide - 1)]
        pairs += [(2 * w + 3, 2 * w + 1) for w in range(0, n_wide - k)]
        held = lax.ppermute(held, ("wide", "rep"), pairs)

        def valid(place, k=k):
            w, r = divmod(place, 2)
            return w >= k if r == 0 else w <= n_wide - 1 - k

        other = lax.ppermute(held, ("groups", "wide", "rep"), swap_pairs(2 * n_wide, valid))
        across = [(p, p ^ 1) for p in range(2 * n_wide) if valid(p)]
        rounds.append(
            (
                held,
                other,
                lax.ppermute(held, ("wide", "rep"), across),
                lax.ppermute(other, ("wide", "rep"), across),
            )
        )
    return rounds


def turn(pieces, tokens):
    return lax.dot_general(
        jnp.concatenate(pieces, axis=0), tokens, (((1,), (1,)), ((), ())), preferred_element_type=jnp.float32
    )


def finish(partial_value, candidate, n_wide, n_layer, chip_seqs):
    wide, layer, rep = (lax.axis_index(a) for a in ("wide", "layer", "rep"))
    n_query = partial_value.shape[0]
    block = n_query // (2 * n_layer)
    part = partial_value.reshape(n_layer, 2, block, n_wide, chip_seqs)
    part = part.reshape(2 * n_layer, block, n_wide, chip_seqs)
    here = 2 * layer + rep
    total = lax.dynamic_index_in_dim(part, here, axis=0, keepdims=False)
    places = 2 * n_layer
    for m in range(1, places):
        shift = [(p, (p + m) % places) for p in range(places)]
        given = lax.dynamic_index_in_dim(part, (here + m) % places, axis=0, keepdims=False)
        total = total + lax.ppermute(given, ("layer", "rep"), shift)
    if n_wide & (n_wide - 1) == 0:
        doubled = jnp.concatenate([total[:, :1], total[:, :0:-1]], axis=1)
        doubled = jnp.concatenate([doubled, doubled], axis=1)
        scores = lax.dynamic_slice_in_dim(doubled, (n_wide - wide) % n_wide, n_wide, axis=1)
        bit = n_wide // 2
        while bit:
            scores = scores.reshape(block, 2, bit, chip_seqs)
            upper = (wide // bit) % 2
            keep = jnp.where(upper == 1, scores[:, 1], scores[:, 0])
            give = jnp.where(upper == 1, scores[:, 0], scores[:, 1])
            scores = keep + lax.ppermute(give, "wide", [(w, w ^ bit) for w in range(n_wide)])
            bit //= 2
        scores = scores.reshape(block, chip_seqs)
    else:
        scores = total[:, 0]
        for n in range(1, n_wide):
            shift = [(w, (w - n) % n_wide) for w in range(n_wide)]
            scores = scores + lax.ppermute(total[:, n], "wide", shift)

    all_seqs = n_wide * chip_seqs
    n_blocks = candidate.shape[1]
    block_size = all_seqs // n_blocks
    seq_index = wide * chip_seqs + jnp.arange(chip_seqs, dtype=jnp.int32)
    one_hot = (seq_index[None, :] // block_size == jnp.arange(n_blocks, dtype=jnp.int32)[:, None]).astype(jnp.float32)
    keep_mask = jnp.dot(candidate.astype(jnp.float32), one_hot, preferred_element_type=jnp.float32)
    return scores * keep_mask


def local(acts, grads, counts, basis_in, basis_out, query_grads, eigenvalues, candidate):
    seq_dev, seq_len, ff_local = acts.shape
    d_local = grads.shape[2]
    n_wide = lax.axis_size("wide")
    n_layer = lax.axis_size("layer")
    group, wide, layer, rep = (lax.axis_index(a) for a in ("groups", "wide", "layer", "rep"))
    n_tok = seq_dev * seq_len
    tok_in = acts.reshape(n_tok, ff_local)
    tok_out = grads.reshape(n_tok, d_local)
    rows_in, rows_out = basis_in.shape[0], basis_out.shape[0]

    def rotate(basis, tokens):
        rows = basis.shape[0]
        half = rows // 2
        own = lax.dynamic_slice_in_dim(basis, group * half, half, axis=0)
        rounds = gather_rounds(own, n_wide)
        slots = [turn([basis], tokens)]
        below, above = {}, {}
        for k, pieces in enumerate(rounds, start=1):
            y = turn(list(pieces), tokens).reshape(2, 2, half, n_tok)
            y = jnp.where(group == 0, y, y[:, ::-1]).reshape(2, rows, n_tok)
            below[k] = jnp.where(rep == 0, y[0], y[1])
            above[k] = jnp.where(rep == 0, y[1], y[0])
        for n in range(1, n_wide):
            slots.append(jnp.where(wide + n <= n_wide - 1, above[n], below[n_wide - n]))
        return jnp.stack(slots)

    grad_part = rotate(basis_out, tok_out).reshape(n_wide * rows_out, n_tok)
    act_part = rotate(basis_in, tok_in).reshape(n_wide * rows_in, n_tok)

    rank_in = n_wide * rows_in
    share = rank_in // n_layer
    doubled = jnp.concatenate([act_part, act_part], axis=0)

    def act_block(owner):
        return lax.dynamic_slice_in_dim(doubled, (owner * share - wide * rows_in) % rank_in, share, axis=0)

    grad_sum = grad_part
    act_sum = act_block(layer)
    grad_sent = grad_part.astype(jnp.bfloat16)
    for m in range(1, n_layer):
        shift = [(i, (i + m) % n_layer) for i in range(n_layer)]
        grad_sum = grad_sum + lax.ppermute(grad_sent, "layer", shift).astype(jnp.float32)
        act_sent = act_block((layer + m) % n_layer).astype(jnp.bfloat16)
        act_sum = act_sum + lax.ppermute(act_sent, "layer", shift).astype(jnp.float32)
    positions = jnp.arange(seq_len, dtype=jnp.int32)
    alive = (positions[None, :] < counts[:, None]).astype(jnp.float32).reshape(n_tok)
    grad_rot = (grad_sum * alive[None, :]).astype(jnp.bfloat16).reshape(n_wide * rows_out, seq_dev, seq_len)
    act_rot = act_sum.astype(jnp.bfloat16).reshape(share, seq_dev, seq_len)
    train = jnp.einsum("gst,ast->sga", grad_rot, act_rot, preferred_element_type=jnp.float32).astype(jnp.bfloat16)

    piece = rows_out // 2
    train = train.reshape(seq_dev, n_wide, 2, piece, share)
    mine = lax.dynamic_index_in_dim(train, rep, axis=2, keepdims=False)
    theirs = lax.ppermute(
        lax.dynamic_index_in_dim(train, 1 - rep, axis=2, keepdims=False), "rep", [(0, 1), (1, 0)]
    )
    both = jnp.stack([jnp.where(rep == 0, mine, theirs), jnp.where(rep == 0, theirs, mine)])
    both = both.reshape(2 * seq_dev, n_wide, piece, share)
    arrived = [both[:, 0]]
    for n in range(1, n_wide):
        shift = [(w, (w + n) % n_wide) for w in range(n_wide)]
        arrived.append(lax.ppermute(both[:, n], "wide", shift))
    chip_seqs = 2 * seq_dev
    train = jnp.stack(arrived).reshape(n_wide * chip_seqs, piece * share)

    n_query = query_grads.shape[0]
    weighted = (query_grads.astype(jnp.float32) / eigenvalues[None, :, :]).astype(jnp.bfloat16)
    weighted = weighted.reshape(n_query, piece * share)
    partial_value = lax.dot_general(weighted, train, (((1,), (1,)), ((), ())), preferred_element_type=jnp.float32)

    return finish(partial_value, candidate, n_wide, n_layer, chip_seqs)


VMEM = pl.BlockSpec(memory_space=pltpu.VMEM)
SMEM = pl.BlockSpec(memory_space=pltpu.SMEM)
ANY = pl.BlockSpec(memory_space=pl.ANY)
FLOAT, HALF = jnp.float32, jnp.bfloat16


def kernel(body, out_shape, scratch=(), flops=0, grant=12):
    return lambda **specs: pl.pallas_call(
        body,
        **specs,
        out_shape=out_shape,
        scratch_shapes=list(scratch),
        compiler_params=pltpu.CompilerParams(vmem_limit_bytes=grant * 1024 * 1024),
        cost_estimate=pl.CostEstimate(flops=flops // 1000, bytes_accessed=1024, transcendentals=0),
    )


def after(value, *earlier):
    return lax.optimization_barrier((value, *earlier))[0]


def run_copies(copies):
    for copy in copies:
        copy.start()
    for copy in copies:
        copy.wait()


def load_body(x_ref, y_ref, x_out, y_out, sems):
    run_copies(
        [pltpu.make_async_copy(x_ref, x_out, sems.at[0]), pltpu.make_async_copy(y_ref, y_out, sems.at[1])]
    )


def sum_of(pieces, start, width, tokens, t_start, total, fresh=True):
    for k in range(0, width, 1024):
        tile = min(1024, width - k)
        rows = [p[:, start + k : start + k + tile] for p in pieces]
        part = lax.dot_general(
            tokens[:, t_start + k : t_start + k + tile],
            jnp.concatenate(rows, axis=0) if len(rows) > 1 else rows[0],
            (((1,), (1,)), ((), ())),
            preferred_element_type=FLOAT,
        )
        if fresh and k == 0:
            total[...] = part
        else:
            total[...] += part


def put(out, place, rows, value):
    out[pl.ds(pl.multiple_of(place * rows, rows), rows), :] = value


def own_body(b_out, b_in, t_out, t_in, g_own, a_own, total):
    sum_of([b_out], 0, b_out.shape[1], t_out, 0, total)
    g_own[...] = total[...].T
    sum_of([b_in], 0, b_in.shape[1], t_in, 0, total)
    a_own[...] = total[...].T


def in_order(group, turned):
    half = turned.shape[0] // 2
    mine, other = turned[:half], turned[half:]
    return jnp.concatenate([jnp.where(group == 0, mine, other), jnp.where(group == 0, other, mine)], axis=0)


def shard_body(flags, at, *refs):
    sources = [refs[2 * i : 2 * i + 2] for i in range(len(flags))]
    t_out, t_in, o_out, o_in, mine, theirs, held, total, sems = refs[2 * len(flags) :]
    d, ff = t_out.shape[1], t_in.shape[1]
    rows = mine.shape[0] // 2
    step = ff // 2 // 128 * 128 + 128
    cuts = [(0, d)] + [(d + k, min(step, ff - k)) for k in range(0, ff, step)]

    def copies(source):
        return [
            [
                pltpu.make_async_copy(p.at[:, pl.ds(*cut)], held.at[j, :, pl.ds(*cut)], sems.at[i, j])
                for j, p in enumerate(source)
            ]
            for i, cut in enumerate(cuts)
        ]

    chosen = at[flags[0]] == 1
    for flag, source in zip(flags, sources, strict=True):
        chosen = chosen | (at[flag] == 1)

        @pl.when(at[flag] == 1)
        def _(source=source):
            for pair in copies(source):
                for copy in pair:
                    copy.start()

    @pl.when(chosen)
    def _():
        waits = copies(sources[0])
        for i, (start, width) in enumerate(cuts):
            for copy in waits[i]:
                copy.wait()
            for j, tokens in enumerate((t_out, o_out) if start < d else (t_in, o_in)):
                first = start if start < d else start - d
                sum_of([held.at[0], held.at[1]], start, width, tokens, first, total.at[j], first == 0)
            if i == 0 or i == len(cuts) - 1:
                put_rows = slice(0, rows) if i == 0 else slice(rows, 2 * rows)
                for j, out in enumerate((mine, theirs)):
                    out[put_rows, :] = in_order(at[0], total[j].T)


def sources_of(at, near, near_far, both, both_far, last, last_far):
    holds, outside = at[4] == 1, at[6] + at[7] == 1
    other, inside = jnp.logical_not(holds), jnp.logical_not(outside)
    return (
        ((near, holds), (near_far, other)),
        ((both, holds), (both_far, other)),
        ((both_far, holds & inside), (both, other & inside), (last, holds & outside), (last_far, other & outside)),
    )


def early_body(at, g_own, a_own, near, near_far, sent):
    rows = g_own.shape[0]
    sent[:rows, :] = g_own[...].astype(HALF)
    sent[rows : 2 * rows, :] = a_own[...].astype(HALF)
    choices = sources_of(at, near, near_far, near, near, near, near)
    for source, condition in choices[0]:

        @pl.when(condition)
        def _(source=source):
            sent[2 * rows :, :] = source[...].astype(HALF)


def late_body(at, both, both_far, last, last_far, sent):
    size = both.shape[0]
    choices = sources_of(at, both, both_far, both, both_far, last, last_far)
    for i, sources in enumerate(choices[1:]):
        for source, condition in sources:

            @pl.when(condition)
            def _(source=source, i=i):
                sent[i * size : (i + 1) * size, :] = source[...].astype(HALF)


def train_body(at, counts, g_own, a_own, near, near_far, both, both_far, last, last_far, early, late, *refs):
    mine, theirs, (grad, act, held) = refs[:4], refs[4:8], refs[8:]
    wide, layer, rep = at[1], at[2], at[3]
    rows, half = g_own.shape[0], mine[0].shape[1]
    near_slot = jnp.where(wide <= 1, 1, 3)

    def place(slot, g, a):
        put(grad, slot, rows, g.astype(HALF))
        shard = lax.rem(wide + slot, 4)
        here = lax.div(shard, 2) == layer

        @pl.when(here)
        def _():
            put(act, lax.rem(shard, 2), rows, a.astype(HALF))

    def came(ref, block):
        return ref[block * rows : (block + 1) * rows, :].astype(FLOAT)

    place(0, g_own[...] + came(early, 0), a_own[...] + came(early, 1))
    choices = sources_of(at, near, near_far, both, both_far, last, last_far)
    for sources, slot, ref, block in zip(choices, (near_slot, 2, 4 - near_slot), (early, late, late), (2, 0, 2), strict=True):
        for source, condition in sources:

            @pl.when(condition)
            def _(source=source, slot=slot, ref=ref, block=block):
                place(slot, source[:rows, :] + came(ref, block), source[rows:, :] + came(ref, block + 1))

    seqs = mine[0].shape[0]
    length = grad.shape[1] // seqs
    spot = lax.broadcasted_iota(jnp.int32, (1, length), 1)
    for s in range(seqs):
        cols = slice(s * length, (s + 1) * length)
        g = jnp.where(spot < counts[s], grad[:, cols].astype(FLOAT), 0.0).astype(HALF)
        held[...] = lax.dot_general(g, act[:, cols], (((1,), (1,)), ((), ())), preferred_element_type=FLOAT).astype(HALF)
        for n in range(4):
            for r, outs in ((rep, mine), (1 - rep, theirs)):
                outs[n][s] = held[pl.ds(pl.multiple_of((2 * n + r) * half, half), half), :]


def score_body(at, weights, *refs):
    same, cross, (out, held, total) = refs[:4], refs[4:8], refs[8:]
    rep = at[3]
    seqs, half = same[0].shape[0], same[0].shape[1]
    for n in range(4):
        for core, pieces in ((rep, same), (1 - rep, cross)):
            for s in range(seqs):
                where = pl.ds(pl.multiple_of(((2 * n + core) * seqs + s) * half, half), half)
                for c in range(held.shape[0]):
                    held[c, where, :] = pieces[n][s][:, c * 128 : (c + 1) * 128].astype(FLOAT)
    count = 8 * seqs
    total[...] = jnp.zeros_like(total)
    for i in range(half):
        block = jnp.concatenate([held[c, pl.ds(i, count, stride=half), :] for c in range(held.shape[0])], axis=1)
        block = block.astype(HALF)
        total[...] += lax.dot_general(weights[i], block, (((1,), (1,)), ((), ())), preferred_element_type=FLOAT)
    out[...] = total[...]


def shaped(*shape, kind=FLOAT):
    return jax.ShapeDtypeStruct(shape, kind)


def local_fast(acts, grads, counts, basis_in, basis_out, query_grads, eigenvalues, candidate):
    n_wide, n_layer = 4, 2
    seq_dev, seq_len, ff = acts.shape
    d = grads.shape[2]
    n_tok = seq_dev * seq_len
    rows = basis_in.shape[0]
    half = rows // 2
    share = n_wide * rows // n_layer
    group, wide, layer, rep = (lax.axis_index(a) for a in ("groups", "wide", "layer", "rep"))
    holds = (rep == 1) == (wide <= 1)
    outside = (wide == 0) | (wide == 3)
    flags = [group, wide, layer, rep, holds, ~holds & ~outside, holds & outside, ~holds & outside]
    at = jnp.stack(flags).astype(jnp.int32)
    swap = [(0, 1), (1, 0)]
    n_query = query_grads.shape[0]
    weighted = (query_grads.astype(FLOAT) / eigenvalues[None, :, :]).astype(HALF).transpose(1, 0, 2)
    dma = pltpu.SemaphoreType.DMA((2,))

    held = jnp.concatenate(
        [lax.dynamic_slice_in_dim(x, group * half, half, axis=0) for x in (basis_out, basis_in)], axis=1
    )

    def load(x, y):
        return kernel(
            load_body, [pltpu.VMEM((n_tok, d), HALF), pltpu.VMEM((n_tok, ff), HALF)], [dma], grant=4
        )(in_specs=[ANY, ANY], out_specs=[VMEM, VMEM])(x.reshape(n_tok, d), y.reshape(n_tok, ff))

    t_out, t_in = load(grads, acts)
    g_own, a_own = kernel(
        own_body, [shaped(rows, n_tok)] * 2, [pltpu.VMEM((n_tok, rows), FLOAT)], 2 * rows * n_tok * (d + ff)
    )(in_specs=[VMEM] * 4, out_specs=[VMEM] * 2)(basis_out, basis_in, t_out, t_in)

    near = [(0, 1), (1, 1), (2, 0), (3, 0)]
    inner = [(1, 0), (2, 1)]
    outer = [(0, 1), (3, 0)]

    def to_group(x, places):
        numbers = {2 * w + r for w, r in places}
        return lax.ppermute(x, ("groups", "wide", "rep"), swap_pairs(2 * n_wide, numbers.__contains__))

    def hop(x, k):
        return lax.ppermute(x, ("wide", "rep"), hop_pairs(k, n_wide))

    o_out, o_in = load(lax.ppermute(grads, "rep", swap), lax.ppermute(acts, "rep", swap))

    def rotate(flags, *pieces):
        both = 2 * rows
        mine, theirs = kernel(
            functools.partial(shard_body, flags),
            [shaped(both, n_tok)] * 2,
            [pltpu.VMEM((2, half, d + ff), HALF), pltpu.VMEM((2, n_tok, rows), FLOAT), pltpu.SemaphoreType.DMA((4, 2))],
            4 * rows * n_tok * (d + ff),
        )(in_specs=[SMEM] + [ANY] * len(pieces) + [VMEM] * 4, out_specs=[VMEM] * 2)(at, *pieces, t_out, t_in, o_out, o_in)
        return mine, lax.ppermute(theirs, "rep", swap)

    x1 = hop(held, 1)
    y1 = to_group(x1, near)
    x1_sent, weighted, _, _ = lax.optimization_barrier((x1, weighted, g_own, a_own))
    x2 = hop(x1_sent, 2)
    x3 = hop(after(x2, y1), 3)
    y2 = to_group(x2, near)
    near_done = rotate([4], x1, y1)
    y3 = to_group(after(x3, y2, near_done[0]), outer)
    y1_inner = to_group(after(x1, y1), inner)
    packed = shaped(4 * rows, n_tok, kind=HALF)
    early = kernel(early_body, packed)(in_specs=[SMEM] + [VMEM] * 4, out_specs=VMEM)(at, g_own, a_own, *near_done)
    early = lax.ppermute(early, "layer", swap)
    both_done = rotate([4, 5], x2, y2, x1, y1_inner)
    last_done = rotate([6], x3, after(y3, both_done[0], early))
    late = kernel(late_body, packed)(in_specs=[SMEM] + [VMEM] * 4, out_specs=VMEM)(at, *both_done, *last_done)
    late = lax.ppermute(late, "layer", swap)

    pieces = kernel(
        train_body,
        [shaped(seq_dev, half, share, kind=HALF)] * 8,
        [pltpu.VMEM((n_wide * rows, n_tok), HALF), pltpu.VMEM((share, n_tok), HALF), pltpu.VMEM((n_wide * rows, share), HALF)],
        2 * n_wide * rows * share * n_tok,
    )(in_specs=[SMEM, SMEM] + [VMEM] * 10, out_specs=[VMEM] * 8)(
        at, counts, g_own, a_own, *near_done, *both_done, *last_done, early, late
    )
    mine, theirs = pieces[:4], pieces[4:]

    def send(x, n, cross):
        pairs = [(2 * w + r, 2 * ((w + n) % n_wide) + (r ^ cross)) for w in range(n_wide) for r in range(2)]
        return lax.ppermute(x, ("wide", "rep"), pairs)

    same = [mine[0]] + [send(mine[n], n, 0) for n in range(1, n_wide)]
    cross = [send(theirs[n], n, 1) for n in range(n_wide)]
    chip_seqs = 2 * seq_dev
    scored = kernel(
        score_body,
        shaped(n_query, n_wide * chip_seqs),
        [pltpu.VMEM((share // 128, n_wide * chip_seqs * half, 128), FLOAT), pltpu.VMEM((n_query, n_wide * chip_seqs), FLOAT)],
        2 * n_query * n_wide * chip_seqs * half * share,
    )(in_specs=[SMEM] + [VMEM] * 9, out_specs=VMEM)(at, weighted, *same, *cross)
    return finish(scored, candidate, n_wide, n_layer, chip_seqs)


def solution(mesh):
    sizes = tuple(mesh.shape[a] for a in ("groups", "wide", "layer", "rep"))
    body = local_fast if sizes == (2, 4, 2, 2) else local
    in_specs = (
        P(("groups", "wide", "rep"), None, "layer"),
        P(("groups", "wide", "rep"), None, "layer"),
        P(("groups", "wide", "rep")),
        P("wide", "layer"),
        P("wide", "layer"),
        P(None, ("wide", "rep"), "layer"),
        P(("wide", "rep"), "layer"),
        P(("layer", "rep"), "groups"),
    )
    out_specs = P(("layer", "rep"), ("groups", "wide"))
    return jax.shard_map(body, mesh=mesh, in_specs=in_specs, out_specs=out_specs, check_vma=False)
```

```python
import functools

import jax
import jax.numpy as jnp
from jax import lax
from jax.experimental import pallas as pl
from jax.experimental.pallas import tpu as pltpu
from jax.sharding import PartitionSpec as P


def swap_pairs(size, valid):
    return [(a * size + k, (1 - a) * size + k) for a in range(2) for k in range(size) if valid(k)]


def hop_pairs(k, n_wide):
    pairs = [(2 * w, 2 * w + 2) for w in range(k - 1, n_wide - 1)]
    return pairs + [(2 * w + 3, 2 * w + 1) for w in range(0, n_wide - k)]


def gather_rounds(own, n_wide):
    rounds = []
    held = own
    for k in range(1, n_wide):
        pairs = [(2 * w, 2 * w + 2) for w in range(k - 1, n_wide - 1)]
        pairs += [(2 * w + 3, 2 * w + 1) for w in range(0, n_wide - k)]
        held = lax.ppermute(held, ("wide", "rep"), pairs)

        def valid(place, k=k):
            w, r = divmod(place, 2)
            return w >= k if r == 0 else w <= n_wide - 1 - k

        other = lax.ppermute(held, ("groups", "wide", "rep"), swap_pairs(2 * n_wide, valid))
        across = [(p, p ^ 1) for p in range(2 * n_wide) if valid(p)]
        rounds.append(
            (
                held,
                other,
                lax.ppermute(held, ("wide", "rep"), across),
                lax.ppermute(other, ("wide", "rep"), across),
            )
        )
    return rounds


def turn(pieces, tokens):
    return lax.dot_general(
        jnp.concatenate(pieces, axis=0), tokens, (((1,), (1,)), ((), ())), preferred_element_type=jnp.float32
    )


def finish(partial_value, candidate, n_wide, n_layer, chip_seqs):
    wide, layer, rep = (lax.axis_index(a) for a in ("wide", "layer", "rep"))
    n_query = partial_value.shape[0]
    block = n_query // (2 * n_layer)
    part = partial_value.reshape(n_layer, 2, block, n_wide, chip_seqs)
    part = part.reshape(2 * n_layer, block, n_wide, chip_seqs)
    here = 2 * layer + rep
    total = lax.dynamic_index_in_dim(part, here, axis=0, keepdims=False)
    places = 2 * n_layer
    for m in range(1, places):
        shift = [(p, (p + m) % places) for p in range(places)]
        given = lax.dynamic_index_in_dim(part, (here + m) % places, axis=0, keepdims=False)
        total = total + lax.ppermute(given, ("layer", "rep"), shift)
    if n_wide & (n_wide - 1) == 0:
        doubled = jnp.concatenate([total[:, :1], total[:, :0:-1]], axis=1)
        doubled = jnp.concatenate([doubled, doubled], axis=1)
        scores = lax.dynamic_slice_in_dim(doubled, (n_wide - wide) % n_wide, n_wide, axis=1)
        bit = n_wide // 2
        while bit:
            scores = scores.reshape(block, 2, bit, chip_seqs)
            upper = (wide // bit) % 2
            keep = jnp.where(upper == 1, scores[:, 1], scores[:, 0])
            give = jnp.where(upper == 1, scores[:, 0], scores[:, 1])
            scores = keep + lax.ppermute(give, "wide", [(w, w ^ bit) for w in range(n_wide)])
            bit //= 2
        scores = scores.reshape(block, chip_seqs)
    else:
        scores = total[:, 0]
        for n in range(1, n_wide):
            shift = [(w, (w - n) % n_wide) for w in range(n_wide)]
            scores = scores + lax.ppermute(total[:, n], "wide", shift)

    all_seqs = n_wide * chip_seqs
    n_blocks = candidate.shape[1]
    block_size = all_seqs // n_blocks
    seq_index = wide * chip_seqs + jnp.arange(chip_seqs, dtype=jnp.int32)
    one_hot = (seq_index[None, :] // block_size == jnp.arange(n_blocks, dtype=jnp.int32)[:, None]).astype(jnp.float32)
    keep_mask = jnp.dot(candidate.astype(jnp.float32), one_hot, preferred_element_type=jnp.float32)
    return scores * keep_mask


def local(acts, grads, counts, basis_in, basis_out, query_grads, eigenvalues, candidate):
    seq_dev, seq_len, ff_local = acts.shape
    d_local = grads.shape[2]
    n_wide = lax.axis_size("wide")
    n_layer = lax.axis_size("layer")
    group, wide, layer, rep = (lax.axis_index(a) for a in ("groups", "wide", "layer", "rep"))
    n_tok = seq_dev * seq_len
    tok_in = acts.reshape(n_tok, ff_local)
    tok_out = grads.reshape(n_tok, d_local)
    rows_in, rows_out = basis_in.shape[0], basis_out.shape[0]

    def rotate(basis, tokens):
        rows = basis.shape[0]
        half = rows // 2
        own = lax.dynamic_slice_in_dim(basis, group * half, half, axis=0)
        rounds = gather_rounds(own, n_wide)
        slots = [turn([basis], tokens)]
        below, above = {}, {}
        for k, pieces in enumerate(rounds, start=1):
            y = turn(list(pieces), tokens).reshape(2, 2, half, n_tok)
            y = jnp.where(group == 0, y, y[:, ::-1]).reshape(2, rows, n_tok)
            below[k] = jnp.where(rep == 0, y[0], y[1])
            above[k] = jnp.where(rep == 0, y[1], y[0])
        for n in range(1, n_wide):
            slots.append(jnp.where(wide + n <= n_wide - 1, above[n], below[n_wide - n]))
        return jnp.stack(slots)

    grad_part = rotate(basis_out, tok_out).reshape(n_wide * rows_out, n_tok)
    act_part = rotate(basis_in, tok_in).reshape(n_wide * rows_in, n_tok)

    rank_in = n_wide * rows_in
    share = rank_in // n_layer
    doubled = jnp.concatenate([act_part, act_part], axis=0)

    def act_block(owner):
        return lax.dynamic_slice_in_dim(doubled, (owner * share - wide * rows_in) % rank_in, share, axis=0)

    grad_sum = grad_part
    act_sum = act_block(layer)
    grad_sent = grad_part.astype(jnp.bfloat16)
    for m in range(1, n_layer):
        shift = [(i, (i + m) % n_layer) for i in range(n_layer)]
        grad_sum = grad_sum + lax.ppermute(grad_sent, "layer", shift).astype(jnp.float32)
        act_sent = act_block((layer + m) % n_layer).astype(jnp.bfloat16)
        act_sum = act_sum + lax.ppermute(act_sent, "layer", shift).astype(jnp.float32)
    positions = jnp.arange(seq_len, dtype=jnp.int32)
    alive = (positions[None, :] < counts[:, None]).astype(jnp.float32).reshape(n_tok)
    grad_rot = (grad_sum * alive[None, :]).astype(jnp.bfloat16).reshape(n_wide * rows_out, seq_dev, seq_len)
    act_rot = act_sum.astype(jnp.bfloat16).reshape(share, seq_dev, seq_len)
    train = jnp.einsum("gst,ast->sga", grad_rot, act_rot, preferred_element_type=jnp.float32).astype(jnp.bfloat16)

    piece = rows_out // 2
    train = train.reshape(seq_dev, n_wide, 2, piece, share)
    mine = lax.dynamic_index_in_dim(train, rep, axis=2, keepdims=False)
    theirs = lax.ppermute(
        lax.dynamic_index_in_dim(train, 1 - rep, axis=2, keepdims=False), "rep", [(0, 1), (1, 0)]
    )
    both = jnp.stack([jnp.where(rep == 0, mine, theirs), jnp.where(rep == 0, theirs, mine)])
    both = both.reshape(2 * seq_dev, n_wide, piece, share)
    arrived = [both[:, 0]]
    for n in range(1, n_wide):
        shift = [(w, (w + n) % n_wide) for w in range(n_wide)]
        arrived.append(lax.ppermute(both[:, n], "wide", shift))
    chip_seqs = 2 * seq_dev
    train = jnp.stack(arrived).reshape(n_wide * chip_seqs, piece * share)

    n_query = query_grads.shape[0]
    weighted = (query_grads.astype(jnp.float32) / eigenvalues[None, :, :]).astype(jnp.bfloat16)
    weighted = weighted.reshape(n_query, piece * share)
    partial_value = lax.dot_general(weighted, train, (((1,), (1,)), ((), ())), preferred_element_type=jnp.float32)

    return finish(partial_value, candidate, n_wide, n_layer, chip_seqs)


VMEM = pl.BlockSpec(memory_space=pltpu.VMEM)
SMEM = pl.BlockSpec(memory_space=pltpu.SMEM)
ANY = pl.BlockSpec(memory_space=pl.ANY)
FLOAT, HALF = jnp.float32, jnp.bfloat16


def kernel(body, out_shape, scratch=(), flops=0, grant=12):
    return lambda **specs: pl.pallas_call(
        body,
        **specs,
        out_shape=out_shape,
        scratch_shapes=list(scratch),
        compiler_params=pltpu.CompilerParams(vmem_limit_bytes=grant * 1024 * 1024),
        cost_estimate=pl.CostEstimate(flops=flops // 1000, bytes_accessed=1024, transcendentals=0),
    )


def after(value, *earlier):
    return lax.optimization_barrier((value, *earlier))[0]


def run_copies(copies):
    for copy in copies:
        copy.start()
    for copy in copies:
        copy.wait()


def load_body(x_ref, y_ref, x_out, y_out, sems):
    run_copies(
        [pltpu.make_async_copy(x_ref, x_out, sems.at[0]), pltpu.make_async_copy(y_ref, y_out, sems.at[1])]
    )


def sum_of(pieces, start, width, tokens, t_start, total, fresh=True):
    for k in range(0, width, 1024):
        tile = min(1024, width - k)
        rows = [p[:, start + k : start + k + tile] for p in pieces]
        part = lax.dot_general(
            tokens[:, t_start + k : t_start + k + tile],
            jnp.concatenate(rows, axis=0) if len(rows) > 1 else rows[0],
            (((1,), (1,)), ((), ())),
            preferred_element_type=FLOAT,
        )
        if fresh and k == 0:
            total[...] = part
        else:
            total[...] += part


def put(out, place, rows, value):
    out[pl.ds(pl.multiple_of(place * rows, rows), rows), :] = value


def own_body(b_out, b_in, t_out, t_in, g_own, a_own, total):
    sum_of([b_out], 0, b_out.shape[1], t_out, 0, total)
    g_own[...] = total[...].T
    sum_of([b_in], 0, b_in.shape[1], t_in, 0, total)
    a_own[...] = total[...].T


def in_order(group, turned):
    half = turned.shape[0] // 2
    mine, other = turned[:half], turned[half:]
    return jnp.concatenate([jnp.where(group == 0, mine, other), jnp.where(group == 0, other, mine)], axis=0)


def shard_body(flags, at, *refs):
    sources = [refs[4 * i : 4 * i + 4] for i in range(len(flags))]
    t_out, t_in, o_out, o_in, mine, theirs, held, total, sems = refs[4 * len(flags) :]
    d, ff = t_out.shape[1], t_in.shape[1]
    rows = mine.shape[0] // 2
    bound = sources[0][0].shape[1]
    middle = (d + ff - bound) // 256 * 128
    cuts = [(0, d), (d, bound - d), (bound, middle), (bound + middle, d + ff - bound - middle)]

    def copies(source):
        pairs = []
        for i, (start, width) in enumerate(cuts):
            part, first = (0, start) if start < bound else (1, start - bound)
            pairs.append(
                [
                    pltpu.make_async_copy(
                        source[2 * j + part].at[:, pl.ds(first, width)], held.at[j, :, pl.ds(start, width)], sems.at[i, j]
                    )
                    for j in range(2)
                ]
            )
        return pairs

    chosen = at[flags[0]] == 1
    for flag, source in zip(flags, sources, strict=True):
        chosen = chosen | (at[flag] == 1)

        @pl.when(at[flag] == 1)
        def _(source=source):
            for pair in copies(source):
                for copy in pair:
                    copy.start()

    @pl.when(chosen)
    def _():
        waits = copies(sources[0])
        for i, (start, width) in enumerate(cuts):
            for copy in waits[i]:
                copy.wait()
            for j, tokens in enumerate((t_out, o_out) if start < d else (t_in, o_in)):
                first = start if start < d else start - d
                sum_of([held.at[0], held.at[1]], start, width, tokens, first, total.at[j], first == 0)
            if i == 0 or i == len(cuts) - 1:
                put_rows = slice(0, rows) if i == 0 else slice(rows, 2 * rows)
                for j, out in enumerate((mine, theirs)):
                    out[put_rows, :] = in_order(at[0], total[j].T)


def sources_of(at, near, near_far, both, both_far, last, last_far):
    holds, outside = at[4] == 1, at[6] + at[7] == 1
    other, inside = jnp.logical_not(holds), jnp.logical_not(outside)
    return (
        ((near, holds), (near_far, other)),
        ((both, holds), (both_far, other)),
        ((both_far, holds & inside), (both, other & inside), (last, holds & outside), (last_far, other & outside)),
    )


def early_body(at, g_own, a_own, near, near_far, sent):
    rows = g_own.shape[0]
    sent[:rows, :] = g_own[...].astype(HALF)
    sent[rows : 2 * rows, :] = a_own[...].astype(HALF)
    choices = sources_of(at, near, near_far, near, near, near, near)
    for source, condition in choices[0]:

        @pl.when(condition)
        def _(source=source):
            sent[2 * rows :, :] = source[...].astype(HALF)


def middle_body(at, both, both_far, sent):
    for source, condition in sources_of(at, both, both_far, both, both_far, both, both)[1]:

        @pl.when(condition)
        def _(source=source):
            sent[...] = source[...].astype(HALF)


def last_body(at, both, both_far, last, last_far, sent):
    for source, condition in sources_of(at, both, both_far, both, both_far, last, last_far)[2]:

        @pl.when(condition)
        def _(source=source):
            sent[...] = source[...].astype(HALF)


def train_body(at, counts, g_own, a_own, near, near_far, both, both_far, last, last_far, early, middle, late, *refs):
    mine, theirs, (grad, act, held) = refs[:4], refs[4:8], refs[8:]
    wide, layer, rep = at[1], at[2], at[3]
    rows, half = g_own.shape[0], mine[0].shape[1]
    near_slot = jnp.where(wide <= 1, 1, 3)

    def place(slot, g, a):
        put(grad, slot, rows, g.astype(HALF))
        shard = lax.rem(wide + slot, 4)
        here = lax.div(shard, 2) == layer

        @pl.when(here)
        def _():
            put(act, lax.rem(shard, 2), rows, a.astype(HALF))

    def came(ref, block):
        return ref[block * rows : (block + 1) * rows, :].astype(FLOAT)

    place(0, g_own[...] + came(early, 0), a_own[...] + came(early, 1))
    choices = sources_of(at, near, near_far, both, both_far, last, last_far)
    for sources, slot, ref, block in zip(choices, (near_slot, 2, 4 - near_slot), (early, middle, late), (2, 0, 0), strict=True):
        for source, condition in sources:

            @pl.when(condition)
            def _(source=source, slot=slot, ref=ref, block=block):
                place(slot, source[:rows, :] + came(ref, block), source[rows:, :] + came(ref, block + 1))

    seqs = mine[0].shape[0]
    length = grad.shape[1] // seqs
    spot = lax.broadcasted_iota(jnp.int32, (1, length), 1)
    for s in range(seqs):
        cols = slice(s * length, (s + 1) * length)
        g = jnp.where(spot < counts[s], grad[:, cols].astype(FLOAT), 0.0).astype(HALF)
        held[...] = lax.dot_general(g, act[:, cols], (((1,), (1,)), ((), ())), preferred_element_type=FLOAT).astype(HALF)
        for n in range(4):
            for r, outs in ((rep, mine), (1 - rep, theirs)):
                outs[n][s] = held[pl.ds(pl.multiple_of((2 * n + r) * half, half), half), :]


def score_body(at, weights, *refs):
    same, cross, (out, held, total) = refs[:4], refs[4:8], refs[8:]
    rep = at[3]
    seqs, half = same[0].shape[0], same[0].shape[1]
    for n in range(4):
        for core, pieces in ((rep, same), (1 - rep, cross)):
            for s in range(seqs):
                where = pl.ds(pl.multiple_of(((2 * n + core) * seqs + s) * half, half), half)
                for c in range(held.shape[0]):
                    held[c, where, :] = pieces[n][s][:, c * 128 : (c + 1) * 128].astype(FLOAT)
    count = 8 * seqs
    total[...] = jnp.zeros_like(total)
    for i in range(half):
        block = jnp.concatenate([held[c, pl.ds(i, count, stride=half), :] for c in range(held.shape[0])], axis=1)
        block = block.astype(HALF)
        total[...] += lax.dot_general(weights[i], block, (((1,), (1,)), ((), ())), preferred_element_type=FLOAT)
    out[...] = total[...]


def shaped(*shape, kind=FLOAT):
    return jax.ShapeDtypeStruct(shape, kind)


def local_fast(acts, grads, counts, basis_in, basis_out, query_grads, eigenvalues, candidate):
    n_wide, n_layer = 4, 2
    seq_dev, seq_len, ff = acts.shape
    d = grads.shape[2]
    n_tok = seq_dev * seq_len
    rows = basis_in.shape[0]
    half = rows // 2
    share = n_wide * rows // n_layer
    group, wide, layer, rep = (lax.axis_index(a) for a in ("groups", "wide", "layer", "rep"))
    holds = (rep == 1) == (wide <= 1)
    outside = (wide == 0) | (wide == 3)
    flags = [group, wide, layer, rep, holds, ~holds & ~outside, holds & outside, ~holds & outside]
    at = jnp.stack(flags).astype(jnp.int32)
    swap = [(0, 1), (1, 0)]
    n_query = query_grads.shape[0]
    weighted = (query_grads.astype(FLOAT) / eigenvalues[None, :, :]).astype(HALF).transpose(1, 0, 2)
    dma = pltpu.SemaphoreType.DMA((2,))

    cut = (ff - d) // 256 * 128
    half_out, half_in = (lax.dynamic_slice_in_dim(x, group * half, half, axis=0) for x in (basis_out, basis_in))
    held = [jnp.concatenate([half_out, half_in[:, :cut]], axis=1), half_in[:, cut:]]

    def load(x, y):
        return kernel(
            load_body, [pltpu.VMEM((n_tok, d), HALF), pltpu.VMEM((n_tok, ff), HALF)], [dma], grant=4
        )(in_specs=[ANY, ANY], out_specs=[VMEM, VMEM])(x.reshape(n_tok, d), y.reshape(n_tok, ff))

    near = [(0, 1), (1, 1), (2, 0), (3, 0)]
    inner = [(1, 0), (2, 1)]
    outer = [(0, 1), (3, 0)]

    def to_group(x, places):
        numbers = {2 * w + r for w, r in places}
        return lax.ppermute(x, ("groups", "wide", "rep"), swap_pairs(2 * n_wide, numbers.__contains__))

    def hop(x, k):
        return lax.ppermute(x, ("wide", "rep"), hop_pairs(k, n_wide))


    x1 = [hop(x, 1) for x in held]
    x2 = [hop(x, 2) for x in x1]
    y1 = [to_group(x, near) for x in x1]
    x3 = [hop(after(x, y), 3) for x, y in zip(x2, y1, strict=True)]

    g_other, a_other = lax.ppermute(grads, "rep", swap), lax.ppermute(acts, "rep", swap)
    own_tokens = [after(x, *x2) for x in (grads, acts)]
    t_out, t_in = load(*own_tokens)
    g_own, a_own = kernel(
        own_body, [shaped(rows, n_tok)] * 2, [pltpu.VMEM((n_tok, rows), FLOAT)], 2 * rows * n_tok * (d + ff)
    )(in_specs=[VMEM] * 4, out_specs=[VMEM] * 2)(basis_out, basis_in, t_out, t_in)

    o_out, o_in = load(g_other, a_other)
    def rotate(flags, *pieces, before=()):
        both = 2 * rows
        mine, theirs = kernel(
            functools.partial(shard_body, flags),
            [shaped(both, n_tok)] * 2,
            [pltpu.VMEM((2, half, d + ff), HALF), pltpu.VMEM((2, n_tok, rows), FLOAT), pltpu.SemaphoreType.DMA((4, 2))],
            4 * rows * n_tok * (d + ff),
        )(in_specs=[SMEM] + [ANY] * len(pieces) + [VMEM] * 4, out_specs=[VMEM] * 2)(at, *pieces, t_out, t_in, o_out, o_in)
        return mine, lax.ppermute(after(theirs, *before), "rep", swap)

    near_done = rotate([4], *x1, *y1)
    y2 = [to_group(x, near) for x in x2]
    y3 = [to_group(x, outer) for x in x3]
    y1_inner = [to_group(after(x, y), inner) for x, y in zip(x1, y1, strict=True)]
    weighted = after(weighted, x3[1])
    early = kernel(early_body, shaped(4 * rows, n_tok, kind=HALF))(in_specs=[SMEM] + [VMEM] * 4, out_specs=VMEM)(
        at, g_own, a_own, *near_done
    )
    early = lax.ppermute(early, "layer", swap)
    both_done = rotate([4, 5], *x2, y2[0], after(y2[1], early), *x1, *y1_inner)
    pair = shaped(2 * rows, n_tok, kind=HALF)
    middle = kernel(middle_body, pair)(in_specs=[SMEM] + [VMEM] * 2, out_specs=VMEM)(at, *both_done)
    middle_came = lax.ppermute(middle, "layer", swap)
    last_done = rotate([6], *x3, y3[0], after(y3[1], middle), before=(middle_came,))
    late = kernel(last_body, pair)(in_specs=[SMEM] + [VMEM] * 4, out_specs=VMEM)(at, *both_done, *last_done)
    late = lax.ppermute(late, "layer", swap)

    pieces = kernel(
        train_body,
        [shaped(seq_dev, half, share, kind=HALF)] * 8,
        [pltpu.VMEM((n_wide * rows, n_tok), HALF), pltpu.VMEM((share, n_tok), HALF), pltpu.VMEM((n_wide * rows, share), HALF)],
        2 * n_wide * rows * share * n_tok,
    )(in_specs=[SMEM, SMEM] + [VMEM] * 11, out_specs=[VMEM] * 8)(
        at, counts, g_own, a_own, *near_done, *both_done, *last_done, early, middle_came, late
    )
    mine, theirs = pieces[:4], pieces[4:]

    def send(x, n, cross):
        pairs = [(2 * w + r, 2 * ((w + n) % n_wide) + (r ^ cross)) for w in range(n_wide) for r in range(2)]
        return lax.ppermute(x, ("wide", "rep"), pairs)

    same = [mine[0]] + [send(mine[n], n, 0) for n in range(1, n_wide)]
    cross = [send(theirs[n], n, 1) for n in range(n_wide)]
    chip_seqs = 2 * seq_dev
    scored = kernel(
        score_body,
        shaped(n_query, n_wide * chip_seqs),
        [pltpu.VMEM((share // 128, n_wide * chip_seqs * half, 128), FLOAT), pltpu.VMEM((n_query, n_wide * chip_seqs), FLOAT)],
        2 * n_query * n_wide * chip_seqs * half * share,
    )(in_specs=[SMEM] + [VMEM] * 9, out_specs=VMEM)(at, weighted, *same, *cross)
    return finish(scored, candidate, n_wide, n_layer, chip_seqs)


def solution(mesh):
    sizes = tuple(mesh.shape[a] for a in ("groups", "wide", "layer", "rep"))
    body = local_fast if sizes == (2, 4, 2, 2) else local
    in_specs = (
        P(("groups", "wide", "rep"), None, "layer"),
        P(("groups", "wide", "rep"), None, "layer"),
        P(("groups", "wide", "rep")),
        P("wide", "layer"),
        P("wide", "layer"),
        P(None, ("wide", "rep"), "layer"),
        P(("wide", "rep"), "layer"),
        P(("layer", "rep"), "groups"),
    )
    out_specs = P(("layer", "rep"), ("groups", "wide"))
    return jax.shard_map(body, mesh=mesh, in_specs=in_specs, out_specs=out_specs, check_vma=False)
```

```python
import functools

import jax
import jax.numpy as jnp
from jax import lax
from jax.experimental import pallas as pl
from jax.experimental.pallas import tpu as pltpu
from jax.sharding import PartitionSpec as P


def swap_pairs(size, valid):
    return [(a * size + k, (1 - a) * size + k) for a in range(2) for k in range(size) if valid(k)]


def hop_pairs(k, n_wide):
    pairs = [(2 * w, 2 * w + 2) for w in range(k - 1, n_wide - 1)]
    return pairs + [(2 * w + 3, 2 * w + 1) for w in range(0, n_wide - k)]


def gather_rounds(own, n_wide):
    rounds = []
    held = own
    for k in range(1, n_wide):
        pairs = [(2 * w, 2 * w + 2) for w in range(k - 1, n_wide - 1)]
        pairs += [(2 * w + 3, 2 * w + 1) for w in range(0, n_wide - k)]
        held = lax.ppermute(held, ("wide", "rep"), pairs)

        def valid(place, k=k):
            w, r = divmod(place, 2)
            return w >= k if r == 0 else w <= n_wide - 1 - k

        other = lax.ppermute(held, ("groups", "wide", "rep"), swap_pairs(2 * n_wide, valid))
        across = [(p, p ^ 1) for p in range(2 * n_wide) if valid(p)]
        rounds.append(
            (
                held,
                other,
                lax.ppermute(held, ("wide", "rep"), across),
                lax.ppermute(other, ("wide", "rep"), across),
            )
        )
    return rounds


def turn(pieces, tokens):
    return lax.dot_general(
        jnp.concatenate(pieces, axis=0), tokens, (((1,), (1,)), ((), ())), preferred_element_type=jnp.float32
    )


def finish(partial_value, candidate, n_wide, n_layer, chip_seqs):
    wide, layer, rep = (lax.axis_index(a) for a in ("wide", "layer", "rep"))
    n_query = partial_value.shape[0]
    block = n_query // (2 * n_layer)
    part = partial_value.reshape(n_layer, 2, block, n_wide, chip_seqs)
    part = part.reshape(2 * n_layer, block, n_wide, chip_seqs)
    here = 2 * layer + rep
    total = lax.dynamic_index_in_dim(part, here, axis=0, keepdims=False)
    places = 2 * n_layer
    for m in range(1, places):
        shift = [(p, (p + m) % places) for p in range(places)]
        given = lax.dynamic_index_in_dim(part, (here + m) % places, axis=0, keepdims=False)
        total = total + lax.ppermute(given, ("layer", "rep"), shift)
    if n_wide & (n_wide - 1) == 0:
        doubled = jnp.concatenate([total[:, :1], total[:, :0:-1]], axis=1)
        doubled = jnp.concatenate([doubled, doubled], axis=1)
        scores = lax.dynamic_slice_in_dim(doubled, (n_wide - wide) % n_wide, n_wide, axis=1)
        bit = n_wide // 2
        while bit:
            scores = scores.reshape(block, 2, bit, chip_seqs)
            upper = (wide // bit) % 2
            keep = jnp.where(upper == 1, scores[:, 1], scores[:, 0])
            give = jnp.where(upper == 1, scores[:, 0], scores[:, 1])
            scores = keep + lax.ppermute(give, "wide", [(w, w ^ bit) for w in range(n_wide)])
            bit //= 2
        scores = scores.reshape(block, chip_seqs)
    else:
        scores = total[:, 0]
        for n in range(1, n_wide):
            shift = [(w, (w - n) % n_wide) for w in range(n_wide)]
            scores = scores + lax.ppermute(total[:, n], "wide", shift)

    all_seqs = n_wide * chip_seqs
    n_blocks = candidate.shape[1]
    block_size = all_seqs // n_blocks
    seq_index = wide * chip_seqs + jnp.arange(chip_seqs, dtype=jnp.int32)
    one_hot = (seq_index[None, :] // block_size == jnp.arange(n_blocks, dtype=jnp.int32)[:, None]).astype(jnp.float32)
    keep_mask = jnp.dot(candidate.astype(jnp.float32), one_hot, preferred_element_type=jnp.float32)
    return scores * keep_mask


def local(acts, grads, counts, basis_in, basis_out, query_grads, eigenvalues, candidate):
    seq_dev, seq_len, ff_local = acts.shape
    d_local = grads.shape[2]
    n_wide = lax.axis_size("wide")
    n_layer = lax.axis_size("layer")
    group, wide, layer, rep = (lax.axis_index(a) for a in ("groups", "wide", "layer", "rep"))
    n_tok = seq_dev * seq_len
    tok_in = acts.reshape(n_tok, ff_local)
    tok_out = grads.reshape(n_tok, d_local)
    rows_in, rows_out = basis_in.shape[0], basis_out.shape[0]

    def rotate(basis, tokens):
        rows = basis.shape[0]
        half = rows // 2
        own = lax.dynamic_slice_in_dim(basis, group * half, half, axis=0)
        rounds = gather_rounds(own, n_wide)
        slots = [turn([basis], tokens)]
        below, above = {}, {}
        for k, pieces in enumerate(rounds, start=1):
            y = turn(list(pieces), tokens).reshape(2, 2, half, n_tok)
            y = jnp.where(group == 0, y, y[:, ::-1]).reshape(2, rows, n_tok)
            below[k] = jnp.where(rep == 0, y[0], y[1])
            above[k] = jnp.where(rep == 0, y[1], y[0])
        for n in range(1, n_wide):
            slots.append(jnp.where(wide + n <= n_wide - 1, above[n], below[n_wide - n]))
        return jnp.stack(slots)

    grad_part = rotate(basis_out, tok_out).reshape(n_wide * rows_out, n_tok)
    act_part = rotate(basis_in, tok_in).reshape(n_wide * rows_in, n_tok)

    rank_in = n_wide * rows_in
    share = rank_in // n_layer
    doubled = jnp.concatenate([act_part, act_part], axis=0)

    def act_block(owner):
        return lax.dynamic_slice_in_dim(doubled, (owner * share - wide * rows_in) % rank_in, share, axis=0)

    grad_sum = grad_part
    act_sum = act_block(layer)
    grad_sent = grad_part.astype(jnp.bfloat16)
    for m in range(1, n_layer):
        shift = [(i, (i + m) % n_layer) for i in range(n_layer)]
        grad_sum = grad_sum + lax.ppermute(grad_sent, "layer", shift).astype(jnp.float32)
        act_sent = act_block((layer + m) % n_layer).astype(jnp.bfloat16)
        act_sum = act_sum + lax.ppermute(act_sent, "layer", shift).astype(jnp.float32)
    positions = jnp.arange(seq_len, dtype=jnp.int32)
    alive = (positions[None, :] < counts[:, None]).astype(jnp.float32).reshape(n_tok)
    grad_rot = (grad_sum * alive[None, :]).astype(jnp.bfloat16).reshape(n_wide * rows_out, seq_dev, seq_len)
    act_rot = act_sum.astype(jnp.bfloat16).reshape(share, seq_dev, seq_len)
    train = jnp.einsum("gst,ast->sga", grad_rot, act_rot, preferred_element_type=jnp.float32).astype(jnp.bfloat16)

    piece = rows_out // 2
    train = train.reshape(seq_dev, n_wide, 2, piece, share)
    mine = lax.dynamic_index_in_dim(train, rep, axis=2, keepdims=False)
    theirs = lax.ppermute(
        lax.dynamic_index_in_dim(train, 1 - rep, axis=2, keepdims=False), "rep", [(0, 1), (1, 0)]
    )
    both = jnp.stack([jnp.where(rep == 0, mine, theirs), jnp.where(rep == 0, theirs, mine)])
    both = both.reshape(2 * seq_dev, n_wide, piece, share)
    arrived = [both[:, 0]]
    for n in range(1, n_wide):
        shift = [(w, (w + n) % n_wide) for w in range(n_wide)]
        arrived.append(lax.ppermute(both[:, n], "wide", shift))
    chip_seqs = 2 * seq_dev
    train = jnp.stack(arrived).reshape(n_wide * chip_seqs, piece * share)

    n_query = query_grads.shape[0]
    weighted = (query_grads.astype(jnp.float32) / eigenvalues[None, :, :]).astype(jnp.bfloat16)
    weighted = weighted.reshape(n_query, piece * share)
    partial_value = lax.dot_general(weighted, train, (((1,), (1,)), ((), ())), preferred_element_type=jnp.float32)

    return finish(partial_value, candidate, n_wide, n_layer, chip_seqs)


VMEM = pl.BlockSpec(memory_space=pltpu.VMEM)
SMEM = pl.BlockSpec(memory_space=pltpu.SMEM)
ANY = pl.BlockSpec(memory_space=pl.ANY)
FLOAT, HALF = jnp.float32, jnp.bfloat16


def kernel(body, out_shape, scratch=(), flops=0, grant=12):
    return lambda **specs: pl.pallas_call(
        body,
        **specs,
        out_shape=out_shape,
        scratch_shapes=list(scratch),
        compiler_params=pltpu.CompilerParams(vmem_limit_bytes=grant * 1024 * 1024),
        cost_estimate=pl.CostEstimate(flops=flops // 1000, bytes_accessed=1024, transcendentals=0),
    )


def after(value, *earlier):
    return lax.optimization_barrier((value, *earlier))[0]


def run_copies(copies):
    for copy in copies:
        copy.start()
    for copy in copies:
        copy.wait()


def load_body(x_ref, y_ref, x_out, y_out, sems):
    run_copies(
        [pltpu.make_async_copy(x_ref, x_out, sems.at[0]), pltpu.make_async_copy(y_ref, y_out, sems.at[1])]
    )


def sum_of(pieces, start, width, tokens, t_start, total, fresh=True):
    for k in range(0, width, 1024):
        tile = min(1024, width - k)
        rows = [p[:, start + k : start + k + tile] for p in pieces]
        part = lax.dot_general(
            tokens[:, t_start + k : t_start + k + tile],
            jnp.concatenate(rows, axis=0) if len(rows) > 1 else rows[0],
            (((1,), (1,)), ((), ())),
            preferred_element_type=FLOAT,
        )
        if fresh and k == 0:
            total[...] = part
        else:
            total[...] += part


def put(out, place, rows, value):
    out[pl.ds(pl.multiple_of(place * rows, rows), rows), :] = value


def own_body(b_out, b_in, t_out, t_in, g_own, a_own, total):
    sum_of([b_out], 0, b_out.shape[1], t_out, 0, total)
    g_own[...] = total[...].T
    sum_of([b_in], 0, b_in.shape[1], t_in, 0, total)
    a_own[...] = total[...].T


def in_order(group, turned):
    half = turned.shape[0] // 2
    mine, other = turned[:half], turned[half:]
    return jnp.concatenate([jnp.where(group == 0, mine, other), jnp.where(group == 0, other, mine)], axis=0)


def shard_body(flags, at, *refs):
    sources = [refs[4 * i : 4 * i + 4] for i in range(len(flags))]
    t_out, t_in, o_out, o_in, mine, theirs, held, total, sems = refs[4 * len(flags) :]
    d, ff = t_out.shape[1], t_in.shape[1]
    rows = mine.shape[0] // 2
    bound = sources[0][0].shape[1]
    middle = (d + ff - bound) // 256 * 128
    cuts = [(0, d), (d, bound - d), (bound, middle), (bound + middle, d + ff - bound - middle)]

    def copies(source):
        pairs = []
        for i, (start, width) in enumerate(cuts):
            part, first = (0, start) if start < bound else (1, start - bound)
            pairs.append(
                [
                    pltpu.make_async_copy(
                        source[2 * j + part].at[:, pl.ds(first, width)], held.at[j, :, pl.ds(start, width)], sems.at[i, j]
                    )
                    for j in range(2)
                ]
            )
        return pairs

    chosen = at[flags[0]] == 1
    for flag, source in zip(flags, sources, strict=True):
        chosen = chosen | (at[flag] == 1)

        @pl.when(at[flag] == 1)
        def _(source=source):
            for pair in copies(source):
                for copy in pair:
                    copy.start()

    @pl.when(chosen)
    def _():
        waits = copies(sources[0])
        for i, (start, width) in enumerate(cuts):
            for copy in waits[i]:
                copy.wait()
            for j, tokens in enumerate((t_out, o_out) if start < d else (t_in, o_in)):
                first = start if start < d else start - d
                sum_of([held.at[0], held.at[1]], start, width, tokens, first, total.at[j], first == 0)
            if i == 0 or i == len(cuts) - 1:
                put_rows = slice(0, rows) if i == 0 else slice(rows, 2 * rows)
                for j, out in enumerate((mine, theirs)):
                    out[put_rows, :] = in_order(at[0], total[j].T)


def sources_of(at, near, near_far, both, both_far, last, last_far):
    holds, outside = at[4] == 1, at[6] + at[7] == 1
    other, inside = jnp.logical_not(holds), jnp.logical_not(outside)
    return (
        ((near, holds), (near_far, other)),
        ((both, holds), (both_far, other)),
        ((both_far, holds & inside), (both, other & inside), (last, holds & outside), (last_far, other & outside)),
    )


def early_body(at, g_own, a_own, near, near_far, sent):
    rows = g_own.shape[0]
    sent[:rows, :] = g_own[...].astype(HALF)
    sent[rows : 2 * rows, :] = a_own[...].astype(HALF)
    choices = sources_of(at, near, near_far, near, near, near, near)
    for source, condition in choices[0]:

        @pl.when(condition)
        def _(source=source):
            sent[2 * rows :, :] = source[...].astype(HALF)


def middle_body(at, both, both_far, sent):
    for source, condition in sources_of(at, both, both_far, both, both_far, both, both)[1]:

        @pl.when(condition)
        def _(source=source):
            sent[...] = source[...].astype(HALF)


def last_body(at, both, both_far, last, last_far, sent):
    for source, condition in sources_of(at, both, both_far, both, both_far, last, last_far)[2]:

        @pl.when(condition)
        def _(source=source):
            sent[...] = source[...].astype(HALF)


def train_body(at, counts, g_own, a_own, near, near_far, both, both_far, last, last_far, early, middle, late, *refs):
    mine, theirs, (grad, act, held) = refs[:4], refs[4:8], refs[8:]
    wide, layer, rep = at[1], at[2], at[3]
    rows, half = g_own.shape[0], mine[0].shape[1]
    near_slot = jnp.where(wide <= 1, 1, 3)

    def place(slot, g, a):
        put(grad, slot, rows, g.astype(HALF))
        shard = lax.rem(wide + slot, 4)
        here = lax.div(shard, 2) == layer

        @pl.when(here)
        def _():
            put(act, lax.rem(shard, 2), rows, a.astype(HALF))

    def came(ref, block):
        return ref[block * rows : (block + 1) * rows, :].astype(FLOAT)

    place(0, g_own[...] + came(early, 0), a_own[...] + came(early, 1))
    choices = sources_of(at, near, near_far, both, both_far, last, last_far)
    for sources, slot, ref, block in zip(choices, (near_slot, 2, 4 - near_slot), (early, middle, late), (2, 0, 0), strict=True):
        for source, condition in sources:

            @pl.when(condition)
            def _(source=source, slot=slot, ref=ref, block=block):
                place(slot, source[:rows, :] + came(ref, block), source[rows:, :] + came(ref, block + 1))

    seqs = mine[0].shape[0]
    length = grad.shape[1] // seqs
    spot = lax.broadcasted_iota(jnp.int32, (1, length), 1)
    for s in range(seqs):
        cols = slice(s * length, (s + 1) * length)
        g = jnp.where(spot < counts[s], grad[:, cols].astype(FLOAT), 0.0).astype(HALF)
        held[...] = lax.dot_general(g, act[:, cols], (((1,), (1,)), ((), ())), preferred_element_type=FLOAT).astype(HALF)
        for n in range(4):
            for r, outs in ((rep, mine), (1 - rep, theirs)):
                outs[n][s] = held[pl.ds(pl.multiple_of((2 * n + r) * half, half), half), :]


def score_body(at, weights, *refs):
    same, cross, (out, held, total) = refs[:4], refs[4:8], refs[8:]
    rep = at[3]
    seqs, half = same[0].shape[0], same[0].shape[1]
    for n in range(4):
        for core, pieces in ((rep, same), (1 - rep, cross)):
            for s in range(seqs):
                where = pl.ds(pl.multiple_of(((2 * n + core) * seqs + s) * half, half), half)
                for c in range(held.shape[0]):
                    held[c, where, :] = pieces[n][s][:, c * 128 : (c + 1) * 128].astype(FLOAT)
    count = 8 * seqs
    total[...] = jnp.zeros_like(total)
    for i in range(half):
        block = jnp.concatenate([held[c, pl.ds(i, count, stride=half), :] for c in range(held.shape[0])], axis=1)
        block = block.astype(HALF)
        total[...] += lax.dot_general(weights[i], block, (((1,), (1,)), ((), ())), preferred_element_type=FLOAT)
    out[...] = total[...]


def shaped(*shape, kind=FLOAT):
    return jax.ShapeDtypeStruct(shape, kind)


def local_fast(acts, grads, counts, basis_in, basis_out, query_grads, eigenvalues, candidate):
    n_wide, n_layer = 4, 2
    seq_dev, seq_len, ff = acts.shape
    d = grads.shape[2]
    n_tok = seq_dev * seq_len
    rows = basis_in.shape[0]
    half = rows // 2
    share = n_wide * rows // n_layer
    group, wide, layer, rep = (lax.axis_index(a) for a in ("groups", "wide", "layer", "rep"))
    holds = (rep == 1) == (wide <= 1)
    outside = (wide == 0) | (wide == 3)
    flags = [group, wide, layer, rep, holds, ~holds & ~outside, holds & outside, ~holds & outside]
    at = jnp.stack(flags).astype(jnp.int32)
    swap = [(0, 1), (1, 0)]
    n_query = query_grads.shape[0]
    weighted = (query_grads.astype(FLOAT) / eigenvalues[None, :, :]).astype(HALF).transpose(1, 0, 2)
    dma = pltpu.SemaphoreType.DMA((2,))

    cut = (ff - d) // 256 * 128
    half_out, half_in = (lax.dynamic_slice_in_dim(x, group * half, half, axis=0) for x in (basis_out, basis_in))
    held = [jnp.concatenate([half_out, half_in[:, :cut]], axis=1), half_in[:, cut:]]

    def load(x, y):
        return kernel(
            load_body, [pltpu.VMEM((n_tok, d), HALF), pltpu.VMEM((n_tok, ff), HALF)], [dma], grant=4
        )(in_specs=[ANY, ANY], out_specs=[VMEM, VMEM])(x.reshape(n_tok, d), y.reshape(n_tok, ff))

    near = [(0, 1), (1, 1), (2, 0), (3, 0)]
    inner = [(1, 0), (2, 1)]
    outer = [(0, 1), (3, 0)]

    def to_group(x, places):
        numbers = {2 * w + r for w, r in places}
        return lax.ppermute(x, ("groups", "wide", "rep"), swap_pairs(2 * n_wide, numbers.__contains__))

    def hop(x, k):
        return lax.ppermute(x, ("wide", "rep"), hop_pairs(k, n_wide))


    x1 = [hop(x, 1) for x in held]
    x2 = [hop(x, 2) for x in x1]
    y1 = [to_group(x, near) for x in x1]
    x3 = [hop(after(x, y), 3) for x, y in zip(x2, y1, strict=True)]

    g_other, a_other = lax.ppermute(grads, "rep", swap), lax.ppermute(acts, "rep", swap)
    own_tokens = [after(x, *x1) for x in (grads, acts)]
    t_out, t_in = load(*own_tokens)
    g_own, a_own = kernel(
        own_body, [shaped(rows, n_tok)] * 2, [pltpu.VMEM((n_tok, rows), FLOAT)], 2 * rows * n_tok * (d + ff)
    )(in_specs=[VMEM] * 4, out_specs=[VMEM] * 2)(basis_out, basis_in, t_out, t_in)

    o_out, o_in = load(g_other, a_other)
    def rotate(flags, *pieces, before=()):
        both = 2 * rows
        mine, theirs = kernel(
            functools.partial(shard_body, flags),
            [shaped(both, n_tok)] * 2,
            [pltpu.VMEM((2, half, d + ff), HALF), pltpu.VMEM((2, n_tok, rows), FLOAT), pltpu.SemaphoreType.DMA((4, 2))],
            4 * rows * n_tok * (d + ff),
        )(in_specs=[SMEM] + [ANY] * len(pieces) + [VMEM] * 4, out_specs=[VMEM] * 2)(at, *pieces, t_out, t_in, o_out, o_in)
        return mine, lax.ppermute(after(theirs, *before), "rep", swap)

    near_done = rotate([4], *x1, *y1)
    y2 = [to_group(x, near) for x in x2]
    y3 = [to_group(x, outer) for x in x3]
    y1_inner = [to_group(after(x, y), inner) for x, y in zip(x1, y1, strict=True)]
    weighted = after(weighted, x3[1])
    early = kernel(early_body, shaped(4 * rows, n_tok, kind=HALF))(in_specs=[SMEM] + [VMEM] * 4, out_specs=VMEM)(
        at, g_own, a_own, *near_done
    )
    early = lax.ppermute(early, "layer", swap)
    both_done = rotate([4, 5], *x2, y2[0], after(y2[1], early), *x1, *y1_inner)
    pair = shaped(2 * rows, n_tok, kind=HALF)
    middle = kernel(middle_body, pair)(in_specs=[SMEM] + [VMEM] * 2, out_specs=VMEM)(at, *both_done)
    middle_came = lax.ppermute(middle, "layer", swap)
    last_done = rotate([6], *x3, y3[0], after(y3[1], middle), before=(middle_came,))
    late = kernel(last_body, pair)(in_specs=[SMEM] + [VMEM] * 4, out_specs=VMEM)(at, *both_done, *last_done)
    late = lax.ppermute(late, "layer", swap)

    pieces = kernel(
        train_body,
        [shaped(seq_dev, half, share, kind=HALF)] * 8,
        [pltpu.VMEM((n_wide * rows, n_tok), HALF), pltpu.VMEM((share, n_tok), HALF), pltpu.VMEM((n_wide * rows, share), HALF)],
        2 * n_wide * rows * share * n_tok,
    )(in_specs=[SMEM, SMEM] + [VMEM] * 11, out_specs=[VMEM] * 8)(
        at, counts, g_own, a_own, *near_done, *both_done, *last_done, early, middle_came, late
    )
    mine, theirs = pieces[:4], pieces[4:]

    def send(x, n, cross):
        pairs = [(2 * w + r, 2 * ((w + n) % n_wide) + (r ^ cross)) for w in range(n_wide) for r in range(2)]
        return lax.ppermute(x, ("wide", "rep"), pairs)

    same = [mine[0]] + [send(mine[n], n, 0) for n in range(1, n_wide)]
    cross = [send(theirs[n], n, 1) for n in range(n_wide)]
    chip_seqs = 2 * seq_dev
    scored = kernel(
        score_body,
        shaped(n_query, n_wide * chip_seqs),
        [pltpu.VMEM((share // 128, n_wide * chip_seqs * half, 128), FLOAT), pltpu.VMEM((n_query, n_wide * chip_seqs), FLOAT)],
        2 * n_query * n_wide * chip_seqs * half * share,
    )(in_specs=[SMEM] + [VMEM] * 9, out_specs=VMEM)(at, weighted, *same, *cross)
    return finish(scored, candidate, n_wide, n_layer, chip_seqs)


def solution(mesh):
    sizes = tuple(mesh.shape[a] for a in ("groups", "wide", "layer", "rep"))
    body = local_fast if sizes == (2, 4, 2, 2) else local
    in_specs = (
        P(("groups", "wide", "rep"), None, "layer"),
        P(("groups", "wide", "rep"), None, "layer"),
        P(("groups", "wide", "rep")),
        P("wide", "layer"),
        P("wide", "layer"),
        P(None, ("wide", "rep"), "layer"),
        P(("wide", "rep"), "layer"),
        P(("layer", "rep"), "groups"),
    )
    out_specs = P(("layer", "rep"), ("groups", "wide"))
    return jax.shard_map(body, mesh=mesh, in_specs=in_specs, out_specs=out_specs, check_vma=False)
```

```python
import functools

import jax
import jax.numpy as jnp
from jax import lax
from jax.experimental import pallas as pl
from jax.experimental.pallas import tpu as pltpu
from jax.sharding import PartitionSpec as P


def swap_pairs(size, valid):
    return [(a * size + k, (1 - a) * size + k) for a in range(2) for k in range(size) if valid(k)]


def hop_pairs(k, n_wide):
    pairs = [(2 * w, 2 * w + 2) for w in range(k - 1, n_wide - 1)]
    return pairs + [(2 * w + 3, 2 * w + 1) for w in range(0, n_wide - k)]


def gather_rounds(own, n_wide):
    rounds = []
    held = own
    for k in range(1, n_wide):
        pairs = [(2 * w, 2 * w + 2) for w in range(k - 1, n_wide - 1)]
        pairs += [(2 * w + 3, 2 * w + 1) for w in range(0, n_wide - k)]
        held = lax.ppermute(held, ("wide", "rep"), pairs)

        def valid(place, k=k):
            w, r = divmod(place, 2)
            return w >= k if r == 0 else w <= n_wide - 1 - k

        other = lax.ppermute(held, ("groups", "wide", "rep"), swap_pairs(2 * n_wide, valid))
        across = [(p, p ^ 1) for p in range(2 * n_wide) if valid(p)]
        rounds.append(
            (
                held,
                other,
                lax.ppermute(held, ("wide", "rep"), across),
                lax.ppermute(other, ("wide", "rep"), across),
            )
        )
    return rounds


def turn(pieces, tokens):
    return lax.dot_general(
        jnp.concatenate(pieces, axis=0), tokens, (((1,), (1,)), ((), ())), preferred_element_type=jnp.float32
    )


def finish(partial_value, candidate, n_wide, n_layer, chip_seqs):
    wide, layer, rep = (lax.axis_index(a) for a in ("wide", "layer", "rep"))
    n_query = partial_value.shape[0]
    block = n_query // (2 * n_layer)
    part = partial_value.reshape(n_layer, 2, block, n_wide, chip_seqs)
    part = part.reshape(2 * n_layer, block, n_wide, chip_seqs)
    here = 2 * layer + rep
    total = lax.dynamic_index_in_dim(part, here, axis=0, keepdims=False)
    places = 2 * n_layer
    for m in range(1, places):
        shift = [(p, (p + m) % places) for p in range(places)]
        given = lax.dynamic_index_in_dim(part, (here + m) % places, axis=0, keepdims=False)
        total = total + lax.ppermute(given, ("layer", "rep"), shift)
    if n_wide & (n_wide - 1) == 0:
        doubled = jnp.concatenate([total[:, :1], total[:, :0:-1]], axis=1)
        doubled = jnp.concatenate([doubled, doubled], axis=1)
        scores = lax.dynamic_slice_in_dim(doubled, (n_wide - wide) % n_wide, n_wide, axis=1)
        bit = n_wide // 2
        while bit:
            scores = scores.reshape(block, 2, bit, chip_seqs)
            upper = (wide // bit) % 2
            keep = jnp.where(upper == 1, scores[:, 1], scores[:, 0])
            give = jnp.where(upper == 1, scores[:, 0], scores[:, 1])
            scores = keep + lax.ppermute(give, "wide", [(w, w ^ bit) for w in range(n_wide)])
            bit //= 2
        scores = scores.reshape(block, chip_seqs)
    else:
        scores = total[:, 0]
        for n in range(1, n_wide):
            shift = [(w, (w - n) % n_wide) for w in range(n_wide)]
            scores = scores + lax.ppermute(total[:, n], "wide", shift)

    all_seqs = n_wide * chip_seqs
    n_blocks = candidate.shape[1]
    block_size = all_seqs // n_blocks
    seq_index = wide * chip_seqs + jnp.arange(chip_seqs, dtype=jnp.int32)
    one_hot = (seq_index[None, :] // block_size == jnp.arange(n_blocks, dtype=jnp.int32)[:, None]).astype(jnp.float32)
    keep_mask = jnp.dot(candidate.astype(jnp.float32), one_hot, preferred_element_type=jnp.float32)
    return scores * keep_mask


def local(acts, grads, counts, basis_in, basis_out, query_grads, eigenvalues, candidate):
    seq_dev, seq_len, ff_local = acts.shape
    d_local = grads.shape[2]
    n_wide = lax.axis_size("wide")
    n_layer = lax.axis_size("layer")
    group, wide, layer, rep = (lax.axis_index(a) for a in ("groups", "wide", "layer", "rep"))
    n_tok = seq_dev * seq_len
    tok_in = acts.reshape(n_tok, ff_local)
    tok_out = grads.reshape(n_tok, d_local)
    rows_in, rows_out = basis_in.shape[0], basis_out.shape[0]

    def rotate(basis, tokens):
        rows = basis.shape[0]
        half = rows // 2
        own = lax.dynamic_slice_in_dim(basis, group * half, half, axis=0)
        rounds = gather_rounds(own, n_wide)
        slots = [turn([basis], tokens)]
        below, above = {}, {}
        for k, pieces in enumerate(rounds, start=1):
            y = turn(list(pieces), tokens).reshape(2, 2, half, n_tok)
            y = jnp.where(group == 0, y, y[:, ::-1]).reshape(2, rows, n_tok)
            below[k] = jnp.where(rep == 0, y[0], y[1])
            above[k] = jnp.where(rep == 0, y[1], y[0])
        for n in range(1, n_wide):
            slots.append(jnp.where(wide + n <= n_wide - 1, above[n], below[n_wide - n]))
        return jnp.stack(slots)

    grad_part = rotate(basis_out, tok_out).reshape(n_wide * rows_out, n_tok)
    act_part = rotate(basis_in, tok_in).reshape(n_wide * rows_in, n_tok)

    rank_in = n_wide * rows_in
    share = rank_in // n_layer
    doubled = jnp.concatenate([act_part, act_part], axis=0)

    def act_block(owner):
        return lax.dynamic_slice_in_dim(doubled, (owner * share - wide * rows_in) % rank_in, share, axis=0)

    grad_sum = grad_part
    act_sum = act_block(layer)
    grad_sent = grad_part.astype(jnp.bfloat16)
    for m in range(1, n_layer):
        shift = [(i, (i + m) % n_layer) for i in range(n_layer)]
        grad_sum = grad_sum + lax.ppermute(grad_sent, "layer", shift).astype(jnp.float32)
        act_sent = act_block((layer + m) % n_layer).astype(jnp.bfloat16)
        act_sum = act_sum + lax.ppermute(act_sent, "layer", shift).astype(jnp.float32)
    positions = jnp.arange(seq_len, dtype=jnp.int32)
    alive = (positions[None, :] < counts[:, None]).astype(jnp.float32).reshape(n_tok)
    grad_rot = (grad_sum * alive[None, :]).astype(jnp.bfloat16).reshape(n_wide * rows_out, seq_dev, seq_len)
    act_rot = act_sum.astype(jnp.bfloat16).reshape(share, seq_dev, seq_len)
    train = jnp.einsum("gst,ast->sga", grad_rot, act_rot, preferred_element_type=jnp.float32).astype(jnp.bfloat16)

    piece = rows_out // 2
    train = train.reshape(seq_dev, n_wide, 2, piece, share)
    mine = lax.dynamic_index_in_dim(train, rep, axis=2, keepdims=False)
    theirs = lax.ppermute(
        lax.dynamic_index_in_dim(train, 1 - rep, axis=2, keepdims=False), "rep", [(0, 1), (1, 0)]
    )
    both = jnp.stack([jnp.where(rep == 0, mine, theirs), jnp.where(rep == 0, theirs, mine)])
    both = both.reshape(2 * seq_dev, n_wide, piece, share)
    arrived = [both[:, 0]]
    for n in range(1, n_wide):
        shift = [(w, (w + n) % n_wide) for w in range(n_wide)]
        arrived.append(lax.ppermute(both[:, n], "wide", shift))
    chip_seqs = 2 * seq_dev
    train = jnp.stack(arrived).reshape(n_wide * chip_seqs, piece * share)

    n_query = query_grads.shape[0]
    weighted = (query_grads.astype(jnp.float32) / eigenvalues[None, :, :]).astype(jnp.bfloat16)
    weighted = weighted.reshape(n_query, piece * share)
    partial_value = lax.dot_general(weighted, train, (((1,), (1,)), ((), ())), preferred_element_type=jnp.float32)

    return finish(partial_value, candidate, n_wide, n_layer, chip_seqs)


VMEM = pl.BlockSpec(memory_space=pltpu.VMEM)
SMEM = pl.BlockSpec(memory_space=pltpu.SMEM)
ANY = pl.BlockSpec(memory_space=pl.ANY)
FLOAT, HALF = jnp.float32, jnp.bfloat16


def kernel(body, out_shape, scratch=(), flops=0, grant=12):
    return lambda **specs: pl.pallas_call(
        body,
        **specs,
        out_shape=out_shape,
        scratch_shapes=list(scratch),
        compiler_params=pltpu.CompilerParams(vmem_limit_bytes=grant * 1024 * 1024),
        cost_estimate=pl.CostEstimate(flops=flops, bytes_accessed=flops // 200, transcendentals=0),
    )


def after(value, *earlier):
    return lax.optimization_barrier((value, *earlier))[0]


def run_copies(copies):
    for copy in copies:
        copy.start()
    for copy in copies:
        copy.wait()


def load_body(x_ref, y_ref, x_out, y_out, sems):
    run_copies(
        [pltpu.make_async_copy(x_ref, x_out, sems.at[0]), pltpu.make_async_copy(y_ref, y_out, sems.at[1])]
    )


def sum_of(pieces, start, width, tokens, t_start, total, fresh=True):
    for k in range(0, width, 1024):
        tile = min(1024, width - k)
        rows = [p[:, start + k : start + k + tile] for p in pieces]
        part = lax.dot_general(
            tokens[:, t_start + k : t_start + k + tile],
            jnp.concatenate(rows, axis=0) if len(rows) > 1 else rows[0],
            (((1,), (1,)), ((), ())),
            preferred_element_type=FLOAT,
        )
        if fresh and k == 0:
            total[...] = part
        else:
            total[...] += part


def put(out, place, rows, value):
    out[pl.ds(pl.multiple_of(place * rows, rows), rows), :] = value


def own_body(b_out, b_in, t_out, t_in, g_own, a_own, total):
    sum_of([b_out], 0, b_out.shape[1], t_out, 0, total)
    g_own[...] = total[...].T
    sum_of([b_in], 0, b_in.shape[1], t_in, 0, total)
    a_own[...] = total[...].T


def in_order(group, turned):
    half = turned.shape[0] // 2
    mine, other = turned[:half], turned[half:]
    return jnp.concatenate([jnp.where(group == 0, mine, other), jnp.where(group == 0, other, mine)], axis=0)


def shard_body(flags, at, *refs):
    sources = [refs[4 * i : 4 * i + 4] for i in range(len(flags))]
    t_out, t_in, o_out, o_in, mine, theirs, held, total, sems = refs[4 * len(flags) :]
    d, ff = t_out.shape[1], t_in.shape[1]
    rows = mine.shape[0] // 2
    bound = sources[0][0].shape[1]
    middle = (d + ff - bound) // 256 * 128
    cuts = [(0, d), (d, bound - d), (bound, middle), (bound + middle, d + ff - bound - middle)]

    def copies(source):
        pairs = []
        for i, (start, width) in enumerate(cuts):
            part, first = (0, start) if start < bound else (1, start - bound)
            pairs.append(
                [
                    pltpu.make_async_copy(
                        source[2 * j + part].at[:, pl.ds(first, width)], held.at[j, :, pl.ds(start, width)], sems.at[i, j]
                    )
                    for j in range(2)
                ]
            )
        return pairs

    chosen = at[flags[0]] == 1
    for flag, source in zip(flags, sources, strict=True):
        chosen = chosen | (at[flag] == 1)

        @pl.when(at[flag] == 1)
        def _(source=source):
            for pair in copies(source):
                for copy in pair:
                    copy.start()

    @pl.when(chosen)
    def _():
        waits = copies(sources[0])
        for i, (start, width) in enumerate(cuts):
            for copy in waits[i]:
                copy.wait()
            for j, tokens in enumerate((t_out, o_out) if start < d else (t_in, o_in)):
                first = start if start < d else start - d
                sum_of([held.at[0], held.at[1]], start, width, tokens, first, total.at[j], first == 0)
            if i == 0 or i == len(cuts) - 1:
                put_rows = slice(0, rows) if i == 0 else slice(rows, 2 * rows)
                for j, out in enumerate((mine, theirs)):
                    out[put_rows, :] = in_order(at[0], total[j].T)


def sources_of(at, near, near_far, both, both_far, last, last_far):
    holds, outside = at[4] == 1, at[6] + at[7] == 1
    other, inside = jnp.logical_not(holds), jnp.logical_not(outside)
    return (
        ((near, holds), (near_far, other)),
        ((both, holds), (both_far, other)),
        ((both_far, holds & inside), (both, other & inside), (last, holds & outside), (last_far, other & outside)),
    )


def early_body(at, g_own, a_own, near, near_far, sent):
    rows = g_own.shape[0]
    sent[:rows, :] = g_own[...].astype(HALF)
    sent[rows : 2 * rows, :] = a_own[...].astype(HALF)
    choices = sources_of(at, near, near_far, near, near, near, near)
    for source, condition in choices[0]:

        @pl.when(condition)
        def _(source=source):
            sent[2 * rows :, :] = source[...].astype(HALF)


def middle_body(at, both, both_far, sent):
    for source, condition in sources_of(at, both, both_far, both, both_far, both, both)[1]:

        @pl.when(condition)
        def _(source=source):
            sent[...] = source[...].astype(HALF)


def last_body(at, both, both_far, last, last_far, sent):
    for source, condition in sources_of(at, both, both_far, both, both_far, last, last_far)[2]:

        @pl.when(condition)
        def _(source=source):
            sent[...] = source[...].astype(HALF)


def train_body(at, counts, g_own, a_own, near, near_far, both, both_far, last, last_far, early, middle, late, *refs):
    mine, theirs, (grad, act, held) = refs[:4], refs[4:8], refs[8:]
    wide, layer, rep = at[1], at[2], at[3]
    rows, half = g_own.shape[0], mine[0].shape[1]
    near_slot = jnp.where(wide <= 1, 1, 3)

    def place(slot, g, a):
        put(grad, slot, rows, g.astype(HALF))
        shard = lax.rem(wide + slot, 4)
        here = lax.div(shard, 2) == layer

        @pl.when(here)
        def _():
            put(act, lax.rem(shard, 2), rows, a.astype(HALF))

    def came(ref, block):
        return ref[block * rows : (block + 1) * rows, :].astype(FLOAT)

    place(0, g_own[...] + came(early, 0), a_own[...] + came(early, 1))
    choices = sources_of(at, near, near_far, both, both_far, last, last_far)
    for sources, slot, ref, block in zip(choices, (near_slot, 2, 4 - near_slot), (early, middle, late), (2, 0, 0), strict=True):
        for source, condition in sources:

            @pl.when(condition)
            def _(source=source, slot=slot, ref=ref, block=block):
                place(slot, source[:rows, :] + came(ref, block), source[rows:, :] + came(ref, block + 1))

    seqs = mine[0].shape[0]
    length = grad.shape[1] // seqs
    spot = lax.broadcasted_iota(jnp.int32, (1, length), 1)
    for s in range(seqs):
        cols = slice(s * length, (s + 1) * length)
        g = jnp.where(spot < counts[s], grad[:, cols].astype(FLOAT), 0.0).astype(HALF)
        held[...] = lax.dot_general(g, act[:, cols], (((1,), (1,)), ((), ())), preferred_element_type=FLOAT).astype(HALF)
        for n in range(4):
            for r, outs in ((rep, mine), (1 - rep, theirs)):
                outs[n][s] = held[pl.ds(pl.multiple_of((2 * n + r) * half, half), half), :]


def score_body(at, weights, *refs):
    same, cross, (out, held, total) = refs[:4], refs[4:8], refs[8:]
    rep = at[3]
    seqs, half = same[0].shape[0], same[0].shape[1]
    for n in range(4):
        for core, pieces in ((rep, same), (1 - rep, cross)):
            for s in range(seqs):
                where = pl.ds(pl.multiple_of(((2 * n + core) * seqs + s) * half, half), half)
                for c in range(held.shape[0]):
                    held[c, where, :] = pieces[n][s][:, c * 128 : (c + 1) * 128].astype(FLOAT)
    count = 8 * seqs
    total[...] = jnp.zeros_like(total)
    for i in range(half):
        block = jnp.concatenate([held[c, pl.ds(i, count, stride=half), :] for c in range(held.shape[0])], axis=1)
        block = block.astype(HALF)
        total[...] += lax.dot_general(weights[i], block, (((1,), (1,)), ((), ())), preferred_element_type=FLOAT)
    out[...] = total[...]


def shaped(*shape, kind=FLOAT):
    return jax.ShapeDtypeStruct(shape, kind)


def local_fast(acts, grads, counts, basis_in, basis_out, query_grads, eigenvalues, candidate):
    n_wide, n_layer = 4, 2
    seq_dev, seq_len, ff = acts.shape
    d = grads.shape[2]
    n_tok = seq_dev * seq_len
    rows = basis_in.shape[0]
    half = rows // 2
    share = n_wide * rows // n_layer
    group, wide, layer, rep = (lax.axis_index(a) for a in ("groups", "wide", "layer", "rep"))
    holds = (rep == 1) == (wide <= 1)
    outside = (wide == 0) | (wide == 3)
    flags = [group, wide, layer, rep, holds, ~holds & ~outside, holds & outside, ~holds & outside]
    at = jnp.stack(flags).astype(jnp.int32)
    swap = [(0, 1), (1, 0)]
    n_query = query_grads.shape[0]
    weighted = (query_grads.astype(FLOAT) / eigenvalues[None, :, :]).astype(HALF).transpose(1, 0, 2)
    dma = pltpu.SemaphoreType.DMA((2,))

    cut = (ff - d) // 256 * 128
    half_out, half_in = (lax.dynamic_slice_in_dim(x, group * half, half, axis=0) for x in (basis_out, basis_in))
    held = [jnp.concatenate([half_out, half_in[:, :cut]], axis=1), half_in[:, cut:]]

    def load(x, y):
        return kernel(
            load_body, [pltpu.VMEM((n_tok, d), HALF), pltpu.VMEM((n_tok, ff), HALF)], [dma], grant=4
        )(in_specs=[ANY, ANY], out_specs=[VMEM, VMEM])(x.reshape(n_tok, d), y.reshape(n_tok, ff))

    near = [(0, 1), (1, 1), (2, 0), (3, 0)]
    inner = [(1, 0), (2, 1)]
    outer = [(0, 1), (3, 0)]

    def to_group(x, places):
        numbers = {2 * w + r for w, r in places}
        return lax.ppermute(x, ("groups", "wide", "rep"), swap_pairs(2 * n_wide, numbers.__contains__))

    def hop(x, k):
        return lax.ppermute(x, ("wide", "rep"), hop_pairs(k, n_wide))


    x1 = [hop(x, 1) for x in held]
    x2 = [hop(x, 2) for x in x1]
    y1 = [to_group(x, near) for x in x1]
    x3 = [hop(after(x, y), 3) for x, y in zip(x2, y1, strict=True)]

    g_other, a_other = lax.ppermute(grads, "rep", swap), lax.ppermute(acts, "rep", swap)
    own_tokens = [after(x, *x1) for x in (grads, acts)]
    t_out, t_in = load(*own_tokens)
    g_own, a_own = kernel(
        own_body, [shaped(rows, n_tok)] * 2, [pltpu.VMEM((n_tok, rows), FLOAT)], 2 * rows * n_tok * (d + ff)
    )(in_specs=[VMEM] * 4, out_specs=[VMEM] * 2)(basis_out, basis_in, t_out, t_in)

    o_out, o_in = load(g_other, a_other)
    def rotate(flags, *pieces, before=()):
        both = 2 * rows
        mine, theirs = kernel(
            functools.partial(shard_body, flags),
            [shaped(both, n_tok)] * 2,
            [pltpu.VMEM((2, half, d + ff), HALF), pltpu.VMEM((2, n_tok, rows), FLOAT), pltpu.SemaphoreType.DMA((4, 2))],
            4 * rows * n_tok * (d + ff),
        )(in_specs=[SMEM] + [ANY] * len(pieces) + [VMEM] * 4, out_specs=[VMEM] * 2)(at, *pieces, t_out, t_in, o_out, o_in)
        return mine, lax.ppermute(after(theirs, *before), "rep", swap)

    near_done = rotate([4], *x1, *y1)
    y2 = [to_group(x, near) for x in x2]
    y3 = [to_group(x, outer) for x in x3]
    y1_inner = [to_group(after(x, y), inner) for x, y in zip(x1, y1, strict=True)]
    weighted = after(weighted, x3[1])
    early = kernel(early_body, shaped(4 * rows, n_tok, kind=HALF))(in_specs=[SMEM] + [VMEM] * 4, out_specs=VMEM)(
        at, g_own, a_own, *near_done
    )
    early = lax.ppermute(early, "layer", swap)
    both_done = rotate([4, 5], *x2, y2[0], after(y2[1], early), *x1, *y1_inner)
    pair = shaped(2 * rows, n_tok, kind=HALF)
    middle = kernel(middle_body, pair)(in_specs=[SMEM] + [VMEM] * 2, out_specs=VMEM)(at, *both_done)
    middle_came = lax.ppermute(middle, "layer", swap)
    last_done = rotate([6], *x3, y3[0], after(y3[1], middle), before=(middle_came,))
    late = kernel(last_body, pair)(in_specs=[SMEM] + [VMEM] * 4, out_specs=VMEM)(at, *both_done, *last_done)
    late = lax.ppermute(late, "layer", swap)

    pieces = kernel(
        train_body,
        [shaped(seq_dev, half, share, kind=HALF)] * 8,
        [pltpu.VMEM((n_wide * rows, n_tok), HALF), pltpu.VMEM((share, n_tok), HALF), pltpu.VMEM((n_wide * rows, share), HALF)],
        2 * n_wide * rows * share * n_tok,
    )(in_specs=[SMEM, SMEM] + [VMEM] * 11, out_specs=[VMEM] * 8)(
        at, counts, g_own, a_own, *near_done, *both_done, *last_done, early, middle_came, late
    )
    mine, theirs = pieces[:4], pieces[4:]

    def send(x, n, cross):
        pairs = [(2 * w + r, 2 * ((w + n) % n_wide) + (r ^ cross)) for w in range(n_wide) for r in range(2)]
        return lax.ppermute(x, ("wide", "rep"), pairs)

    same = [mine[0]] + [send(mine[n], n, 0) for n in range(1, n_wide)]
    cross = [send(theirs[n], n, 1) for n in range(n_wide)]
    chip_seqs = 2 * seq_dev
    scored = kernel(
        score_body,
        shaped(n_query, n_wide * chip_seqs),
        [pltpu.VMEM((share // 128, n_wide * chip_seqs * half, 128), FLOAT), pltpu.VMEM((n_query, n_wide * chip_seqs), FLOAT)],
        2 * n_query * n_wide * chip_seqs * half * share,
    )(in_specs=[SMEM] + [VMEM] * 9, out_specs=VMEM)(at, weighted, *same, *cross)
    return finish(scored, candidate, n_wide, n_layer, chip_seqs)


def solution(mesh):
    sizes = tuple(mesh.shape[a] for a in ("groups", "wide", "layer", "rep"))
    body = local_fast if sizes == (2, 4, 2, 2) else local
    in_specs = (
        P(("groups", "wide", "rep"), None, "layer"),
        P(("groups", "wide", "rep"), None, "layer"),
        P(("groups", "wide", "rep")),
        P("wide", "layer"),
        P("wide", "layer"),
        P(None, ("wide", "rep"), "layer"),
        P(("wide", "rep"), "layer"),
        P(("layer", "rep"), "groups"),
    )
    out_specs = P(("layer", "rep"), ("groups", "wide"))
    return jax.shard_map(body, mesh=mesh, in_specs=in_specs, out_specs=out_specs, check_vma=False)
```

```python
import functools

import jax
import jax.numpy as jnp
from jax import lax
from jax.experimental import pallas as pl
from jax.experimental.pallas import tpu as pltpu
from jax.sharding import PartitionSpec as P


def swap_pairs(size, valid):
    return [(a * size + k, (1 - a) * size + k) for a in range(2) for k in range(size) if valid(k)]


def hop_pairs(k, n_wide):
    pairs = [(2 * w, 2 * w + 2) for w in range(k - 1, n_wide - 1)]
    return pairs + [(2 * w + 3, 2 * w + 1) for w in range(0, n_wide - k)]


def gather_rounds(own, n_wide):
    rounds = []
    held = own
    for k in range(1, n_wide):
        pairs = [(2 * w, 2 * w + 2) for w in range(k - 1, n_wide - 1)]
        pairs += [(2 * w + 3, 2 * w + 1) for w in range(0, n_wide - k)]
        held = lax.ppermute(held, ("wide", "rep"), pairs)

        def valid(place, k=k):
            w, r = divmod(place, 2)
            return w >= k if r == 0 else w <= n_wide - 1 - k

        other = lax.ppermute(held, ("groups", "wide", "rep"), swap_pairs(2 * n_wide, valid))
        across = [(p, p ^ 1) for p in range(2 * n_wide) if valid(p)]
        rounds.append(
            (
                held,
                other,
                lax.ppermute(held, ("wide", "rep"), across),
                lax.ppermute(other, ("wide", "rep"), across),
            )
        )
    return rounds


def turn(pieces, tokens):
    return lax.dot_general(
        jnp.concatenate(pieces, axis=0), tokens, (((1,), (1,)), ((), ())), preferred_element_type=jnp.float32
    )


def finish(partial_value, candidate, n_wide, n_layer, chip_seqs):
    wide, layer, rep = (lax.axis_index(a) for a in ("wide", "layer", "rep"))
    n_query = partial_value.shape[0]
    block = n_query // (2 * n_layer)
    part = partial_value.reshape(n_layer, 2, block, n_wide, chip_seqs)
    part = part.reshape(2 * n_layer, block, n_wide, chip_seqs)
    here = 2 * layer + rep
    total = lax.dynamic_index_in_dim(part, here, axis=0, keepdims=False)
    places = 2 * n_layer
    for m in range(1, places):
        shift = [(p, (p + m) % places) for p in range(places)]
        given = lax.dynamic_index_in_dim(part, (here + m) % places, axis=0, keepdims=False)
        total = total + lax.ppermute(given, ("layer", "rep"), shift)
    if n_wide & (n_wide - 1) == 0:
        doubled = jnp.concatenate([total[:, :1], total[:, :0:-1]], axis=1)
        doubled = jnp.concatenate([doubled, doubled], axis=1)
        scores = lax.dynamic_slice_in_dim(doubled, (n_wide - wide) % n_wide, n_wide, axis=1)
        bit = n_wide // 2
        while bit:
            scores = scores.reshape(block, 2, bit, chip_seqs)
            upper = (wide // bit) % 2
            keep = jnp.where(upper == 1, scores[:, 1], scores[:, 0])
            give = jnp.where(upper == 1, scores[:, 0], scores[:, 1])
            scores = keep + lax.ppermute(give, "wide", [(w, w ^ bit) for w in range(n_wide)])
            bit //= 2
        scores = scores.reshape(block, chip_seqs)
    else:
        scores = total[:, 0]
        for n in range(1, n_wide):
            shift = [(w, (w - n) % n_wide) for w in range(n_wide)]
            scores = scores + lax.ppermute(total[:, n], "wide", shift)

    all_seqs = n_wide * chip_seqs
    n_blocks = candidate.shape[1]
    block_size = all_seqs // n_blocks
    seq_index = wide * chip_seqs + jnp.arange(chip_seqs, dtype=jnp.int32)
    one_hot = (seq_index[None, :] // block_size == jnp.arange(n_blocks, dtype=jnp.int32)[:, None]).astype(jnp.float32)
    keep_mask = jnp.dot(candidate.astype(jnp.float32), one_hot, preferred_element_type=jnp.float32)
    return scores * keep_mask


def local(acts, grads, counts, basis_in, basis_out, query_grads, eigenvalues, candidate):
    seq_dev, seq_len, ff_local = acts.shape
    d_local = grads.shape[2]
    n_wide = lax.axis_size("wide")
    n_layer = lax.axis_size("layer")
    group, wide, layer, rep = (lax.axis_index(a) for a in ("groups", "wide", "layer", "rep"))
    n_tok = seq_dev * seq_len
    tok_in = acts.reshape(n_tok, ff_local)
    tok_out = grads.reshape(n_tok, d_local)
    rows_in, rows_out = basis_in.shape[0], basis_out.shape[0]

    def rotate(basis, tokens):
        rows = basis.shape[0]
        half = rows // 2
        own = lax.dynamic_slice_in_dim(basis, group * half, half, axis=0)
        rounds = gather_rounds(own, n_wide)
        slots = [turn([basis], tokens)]
        below, above = {}, {}
        for k, pieces in enumerate(rounds, start=1):
            y = turn(list(pieces), tokens).reshape(2, 2, half, n_tok)
            y = jnp.where(group == 0, y, y[:, ::-1]).reshape(2, rows, n_tok)
            below[k] = jnp.where(rep == 0, y[0], y[1])
            above[k] = jnp.where(rep == 0, y[1], y[0])
        for n in range(1, n_wide):
            slots.append(jnp.where(wide + n <= n_wide - 1, above[n], below[n_wide - n]))
        return jnp.stack(slots)

    grad_part = rotate(basis_out, tok_out).reshape(n_wide * rows_out, n_tok)
    act_part = rotate(basis_in, tok_in).reshape(n_wide * rows_in, n_tok)

    rank_in = n_wide * rows_in
    share = rank_in // n_layer
    doubled = jnp.concatenate([act_part, act_part], axis=0)

    def act_block(owner):
        return lax.dynamic_slice_in_dim(doubled, (owner * share - wide * rows_in) % rank_in, share, axis=0)

    grad_sum = grad_part
    act_sum = act_block(layer)
    grad_sent = grad_part.astype(jnp.bfloat16)
    for m in range(1, n_layer):
        shift = [(i, (i + m) % n_layer) for i in range(n_layer)]
        grad_sum = grad_sum + lax.ppermute(grad_sent, "layer", shift).astype(jnp.float32)
        act_sent = act_block((layer + m) % n_layer).astype(jnp.bfloat16)
        act_sum = act_sum + lax.ppermute(act_sent, "layer", shift).astype(jnp.float32)
    positions = jnp.arange(seq_len, dtype=jnp.int32)
    alive = (positions[None, :] < counts[:, None]).astype(jnp.float32).reshape(n_tok)
    grad_rot = (grad_sum * alive[None, :]).astype(jnp.bfloat16).reshape(n_wide * rows_out, seq_dev, seq_len)
    act_rot = act_sum.astype(jnp.bfloat16).reshape(share, seq_dev, seq_len)
    train = jnp.einsum("gst,ast->sga", grad_rot, act_rot, preferred_element_type=jnp.float32).astype(jnp.bfloat16)

    piece = rows_out // 2
    train = train.reshape(seq_dev, n_wide, 2, piece, share)
    mine = lax.dynamic_index_in_dim(train, rep, axis=2, keepdims=False)
    theirs = lax.ppermute(
        lax.dynamic_index_in_dim(train, 1 - rep, axis=2, keepdims=False), "rep", [(0, 1), (1, 0)]
    )
    both = jnp.stack([jnp.where(rep == 0, mine, theirs), jnp.where(rep == 0, theirs, mine)])
    both = both.reshape(2 * seq_dev, n_wide, piece, share)
    arrived = [both[:, 0]]
    for n in range(1, n_wide):
        shift = [(w, (w + n) % n_wide) for w in range(n_wide)]
        arrived.append(lax.ppermute(both[:, n], "wide", shift))
    chip_seqs = 2 * seq_dev
    train = jnp.stack(arrived).reshape(n_wide * chip_seqs, piece * share)

    n_query = query_grads.shape[0]
    weighted = (query_grads.astype(jnp.float32) / eigenvalues[None, :, :]).astype(jnp.bfloat16)
    weighted = weighted.reshape(n_query, piece * share)
    partial_value = lax.dot_general(weighted, train, (((1,), (1,)), ((), ())), preferred_element_type=jnp.float32)

    return finish(partial_value, candidate, n_wide, n_layer, chip_seqs)


VMEM = pl.BlockSpec(memory_space=pltpu.VMEM)
SMEM = pl.BlockSpec(memory_space=pltpu.SMEM)
ANY = pl.BlockSpec(memory_space=pl.ANY)
FLOAT, HALF = jnp.float32, jnp.bfloat16


def kernel(body, out_shape, scratch=(), flops=0, grant=12):
    return lambda **specs: pl.pallas_call(
        body,
        **specs,
        out_shape=out_shape,
        scratch_shapes=list(scratch),
        compiler_params=pltpu.CompilerParams(vmem_limit_bytes=grant * 1024 * 1024),
        cost_estimate=pl.CostEstimate(flops=flops, bytes_accessed=flops // 200, transcendentals=0),
    )


def after(value, *earlier):
    return lax.optimization_barrier((value, *earlier))[0]


def run_copies(copies):
    for copy in copies:
        copy.start()
    for copy in copies:
        copy.wait()


def load_body(x_ref, y_ref, x_out, y_out, sems):
    run_copies(
        [pltpu.make_async_copy(x_ref, x_out, sems.at[0]), pltpu.make_async_copy(y_ref, y_out, sems.at[1])]
    )


def sum_of(pieces, start, width, tokens, t_start, total, fresh=True):
    for k in range(0, width, 1024):
        tile = min(1024, width - k)
        rows = [p[:, start + k : start + k + tile] for p in pieces]
        part = lax.dot_general(
            tokens[:, t_start + k : t_start + k + tile],
            jnp.concatenate(rows, axis=0) if len(rows) > 1 else rows[0],
            (((1,), (1,)), ((), ())),
            preferred_element_type=FLOAT,
        )
        if fresh and k == 0:
            total[...] = part
        else:
            total[...] += part


def put(out, place, rows, value):
    out[pl.ds(pl.multiple_of(place * rows, rows), rows), :] = value


def own_body(b_out, b_in, t_out, t_in, g_own, a_own, total):
    sum_of([b_out], 0, b_out.shape[1], t_out, 0, total)
    g_own[...] = total[...].T
    sum_of([b_in], 0, b_in.shape[1], t_in, 0, total)
    a_own[...] = total[...].T


def in_order(group, turned):
    half = turned.shape[0] // 2
    mine, other = turned[:half], turned[half:]
    return jnp.concatenate([jnp.where(group == 0, mine, other), jnp.where(group == 0, other, mine)], axis=0)


def shard_body(flags, at, *refs):
    sources = [refs[4 * i : 4 * i + 4] for i in range(len(flags))]
    t_out, t_in, o_out, o_in, mine, theirs, held, total, sems = refs[4 * len(flags) :]
    d, ff = t_out.shape[1], t_in.shape[1]
    rows = mine.shape[0] // 2
    bound = sources[0][0].shape[1]
    middle = (d + ff - bound) // 256 * 128
    cuts = [(0, d), (d, bound - d), (bound, middle), (bound + middle, d + ff - bound - middle)]

    def copies(source):
        pairs = []
        for i, (start, width) in enumerate(cuts):
            part, first = (0, start) if start < bound else (1, start - bound)
            pairs.append(
                [
                    pltpu.make_async_copy(
                        source[2 * j + part].at[:, pl.ds(first, width)], held.at[j, :, pl.ds(start, width)], sems.at[i, j]
                    )
                    for j in range(2)
                ]
            )
        return pairs

    chosen = at[flags[0]] == 1
    for flag, source in zip(flags, sources, strict=True):
        chosen = chosen | (at[flag] == 1)

        @pl.when(at[flag] == 1)
        def _(source=source):
            for pair in copies(source):
                for copy in pair:
                    copy.start()

    @pl.when(chosen)
    def _():
        waits = copies(sources[0])
        for i, (start, width) in enumerate(cuts):
            for copy in waits[i]:
                copy.wait()
            for j, tokens in enumerate((t_out, o_out) if start < d else (t_in, o_in)):
                first = start if start < d else start - d
                sum_of([held.at[0], held.at[1]], start, width, tokens, first, total.at[j], first == 0)
            if i == 0 or i == len(cuts) - 1:
                put_rows = slice(0, rows) if i == 0 else slice(rows, 2 * rows)
                for j, out in enumerate((mine, theirs)):
                    out[put_rows, :] = in_order(at[0], total[j].T)


def sources_of(at, near, near_far, both, both_far, last, last_far):
    holds, outside = at[4] == 1, at[6] + at[7] == 1
    other, inside = jnp.logical_not(holds), jnp.logical_not(outside)
    return (
        ((near, holds), (near_far, other)),
        ((both, holds), (both_far, other)),
        ((both_far, holds & inside), (both, other & inside), (last, holds & outside), (last_far, other & outside)),
    )


def early_body(at, g_own, a_own, near, near_far, sent):
    rows = g_own.shape[0]
    sent[:rows, :] = g_own[...].astype(HALF)
    sent[rows : 2 * rows, :] = a_own[...].astype(HALF)
    choices = sources_of(at, near, near_far, near, near, near, near)
    for source, condition in choices[0]:

        @pl.when(condition)
        def _(source=source):
            sent[2 * rows :, :] = source[...].astype(HALF)


def middle_body(at, both, both_far, sent):
    for source, condition in sources_of(at, both, both_far, both, both_far, both, both)[1]:

        @pl.when(condition)
        def _(source=source):
            sent[...] = source[...].astype(HALF)


def last_body(at, both, both_far, last, last_far, sent):
    for source, condition in sources_of(at, both, both_far, both, both_far, last, last_far)[2]:

        @pl.when(condition)
        def _(source=source):
            sent[...] = source[...].astype(HALF)


def train_body(at, counts, g_own, a_own, near, near_far, both, both_far, last, last_far, early, middle, late, *refs):
    mine, theirs, (grad, act, held) = refs[:4], refs[4:8], refs[8:]
    wide, layer, rep = at[1], at[2], at[3]
    rows, half = g_own.shape[0], mine[0].shape[1]
    near_slot = jnp.where(wide <= 1, 1, 3)

    def place(slot, g, a):
        put(grad, slot, rows, g.astype(HALF))
        shard = lax.rem(wide + slot, 4)
        here = lax.div(shard, 2) == layer

        @pl.when(here)
        def _():
            put(act, lax.rem(shard, 2), rows, a.astype(HALF))

    def came(ref, block):
        return ref[block * rows : (block + 1) * rows, :].astype(FLOAT)

    place(0, g_own[...] + came(early, 0), a_own[...] + came(early, 1))
    choices = sources_of(at, near, near_far, both, both_far, last, last_far)
    for sources, slot, ref, block in zip(choices, (near_slot, 2, 4 - near_slot), (early, middle, late), (2, 0, 0), strict=True):
        for source, condition in sources:

            @pl.when(condition)
            def _(source=source, slot=slot, ref=ref, block=block):
                place(slot, source[:rows, :] + came(ref, block), source[rows:, :] + came(ref, block + 1))

    seqs = mine[0].shape[0]
    length = grad.shape[1] // seqs
    spot = lax.broadcasted_iota(jnp.int32, (1, length), 1)
    for s in range(seqs):
        cols = slice(s * length, (s + 1) * length)
        g = jnp.where(spot < counts[s], grad[:, cols].astype(FLOAT), 0.0).astype(HALF)
        held[...] = lax.dot_general(g, act[:, cols], (((1,), (1,)), ((), ())), preferred_element_type=FLOAT).astype(HALF)
        for n in range(4):
            for r, outs in ((rep, mine), (1 - rep, theirs)):
                outs[n][s] = held[pl.ds(pl.multiple_of((2 * n + r) * half, half), half), :]


def score_body(at, weights, *refs):
    same, cross, (out, held, total) = refs[:4], refs[4:8], refs[8:]
    rep = at[3]
    seqs, half = same[0].shape[0], same[0].shape[1]
    for n in range(4):
        for core, pieces in ((rep, same), (1 - rep, cross)):
            for s in range(seqs):
                where = pl.ds(pl.multiple_of(((2 * n + core) * seqs + s) * half, half), half)
                for c in range(held.shape[0]):
                    held[c, where, :] = pieces[n][s][:, c * 128 : (c + 1) * 128].astype(FLOAT)
    count = 8 * seqs
    total[...] = jnp.zeros_like(total)
    for i in range(half):
        block = jnp.concatenate([held[c, pl.ds(i, count, stride=half), :] for c in range(held.shape[0])], axis=1)
        block = block.astype(HALF)
        total[...] += lax.dot_general(weights[i], block, (((1,), (1,)), ((), ())), preferred_element_type=FLOAT)
    out[...] = total[...]


def shaped(*shape, kind=FLOAT):
    return jax.ShapeDtypeStruct(shape, kind)


def local_fast(acts, grads, counts, basis_in, basis_out, query_grads, eigenvalues, candidate):
    n_wide, n_layer = 4, 2
    seq_dev, seq_len, ff = acts.shape
    d = grads.shape[2]
    n_tok = seq_dev * seq_len
    rows = basis_in.shape[0]
    half = rows // 2
    share = n_wide * rows // n_layer
    group, wide, layer, rep = (lax.axis_index(a) for a in ("groups", "wide", "layer", "rep"))
    holds = (rep == 1) == (wide <= 1)
    outside = (wide == 0) | (wide == 3)
    flags = [group, wide, layer, rep, holds, ~holds & ~outside, holds & outside, ~holds & outside]
    at = jnp.stack(flags).astype(jnp.int32)
    swap = [(0, 1), (1, 0)]
    n_query = query_grads.shape[0]
    weighted = (query_grads.astype(FLOAT) / eigenvalues[None, :, :]).astype(HALF).transpose(1, 0, 2)
    dma = pltpu.SemaphoreType.DMA((2,))

    cut = (ff - d) // 256 * 128
    half_out, half_in = (lax.dynamic_slice_in_dim(x, group * half, half, axis=0) for x in (basis_out, basis_in))
    held = [jnp.concatenate([half_out, half_in[:, :cut]], axis=1), half_in[:, cut:]]

    def load(x, y):
        return kernel(
            load_body, [pltpu.VMEM((n_tok, d), HALF), pltpu.VMEM((n_tok, ff), HALF)], [dma], grant=4
        )(in_specs=[ANY, ANY], out_specs=[VMEM, VMEM])(x.reshape(n_tok, d), y.reshape(n_tok, ff))

    near = [(0, 1), (1, 1), (2, 0), (3, 0)]
    inner = [(1, 0), (2, 1)]
    outer = [(0, 1), (3, 0)]

    def to_group(x, places):
        numbers = {2 * w + r for w, r in places}
        return lax.ppermute(x, ("groups", "wide", "rep"), swap_pairs(2 * n_wide, numbers.__contains__))

    def hop(x, k):
        return lax.ppermute(x, ("wide", "rep"), hop_pairs(k, n_wide))


    x1 = [hop(x, 1) for x in held]
    x2 = [hop(x, 2) for x in x1]
    y1 = [to_group(x, near) for x in x1]
    x3 = [hop(after(x, y), 3) for x, y in zip(x2, y1, strict=True)]

    g_other, a_other = lax.ppermute(grads, "rep", swap), lax.ppermute(acts, "rep", swap)
    own_tokens = [after(x, *x1) for x in (grads, acts)]
    t_out, t_in = load(*own_tokens)
    g_own, a_own = kernel(
        own_body, [shaped(rows, n_tok)] * 2, [pltpu.VMEM((n_tok, rows), FLOAT)], 2 * rows * n_tok * (d + ff)
    )(in_specs=[VMEM] * 4, out_specs=[VMEM] * 2)(basis_out, basis_in, t_out, t_in)

    o_out, o_in = load(g_other, a_other)
    def rotate(flags, *pieces, before=()):
        both = 2 * rows
        mine, theirs = kernel(
            functools.partial(shard_body, flags),
            [shaped(both, n_tok)] * 2,
            [pltpu.VMEM((2, half, d + ff), HALF), pltpu.VMEM((2, n_tok, rows), FLOAT), pltpu.SemaphoreType.DMA((4, 2))],
            4 * rows * n_tok * (d + ff),
        )(in_specs=[SMEM] + [ANY] * len(pieces) + [VMEM] * 4, out_specs=[VMEM] * 2)(at, *pieces, t_out, t_in, o_out, o_in)
        return mine, lax.ppermute(after(theirs, *before), "rep", swap)

    near_done = rotate([4], *x1, *y1)
    y2 = [to_group(x, near) for x in x2]
    y3 = [to_group(x, outer) for x in x3]
    y1_inner = [to_group(after(x, y), inner) for x, y in zip(x1, y1, strict=True)]
    weighted = after(weighted, x3[1])
    early = kernel(early_body, shaped(4 * rows, n_tok, kind=HALF))(in_specs=[SMEM] + [VMEM] * 4, out_specs=VMEM)(
        at, g_own, a_own, *near_done
    )
    early = lax.ppermute(early, "layer", swap)
    both_done = rotate([4, 5], *x2, y2[0], after(y2[1], near_done[0]), *x1, *y1_inner)
    pair = shaped(2 * rows, n_tok, kind=HALF)
    middle = kernel(middle_body, pair)(in_specs=[SMEM] + [VMEM] * 2, out_specs=VMEM)(at, *both_done)
    middle_came = lax.ppermute(middle, "layer", swap)
    last_done = rotate([6], *x3, y3[0], after(y3[1], middle), before=(middle_came, early))
    late = kernel(last_body, pair)(in_specs=[SMEM] + [VMEM] * 4, out_specs=VMEM)(at, *both_done, *last_done)
    late = lax.ppermute(late, "layer", swap)

    pieces = kernel(
        train_body,
        [shaped(seq_dev, half, share, kind=HALF)] * 8,
        [pltpu.VMEM((n_wide * rows, n_tok), HALF), pltpu.VMEM((share, n_tok), HALF), pltpu.VMEM((n_wide * rows, share), HALF)],
        2 * n_wide * rows * share * n_tok,
    )(in_specs=[SMEM, SMEM] + [VMEM] * 11, out_specs=[VMEM] * 8)(
        at, counts, g_own, a_own, *near_done, *both_done, *last_done, early, middle_came, late
    )
    mine, theirs = pieces[:4], pieces[4:]

    def send(x, n, cross):
        pairs = [(2 * w + r, 2 * ((w + n) % n_wide) + (r ^ cross)) for w in range(n_wide) for r in range(2)]
        return lax.ppermute(x, ("wide", "rep"), pairs)

    same = [mine[0]] + [send(mine[n], n, 0) for n in range(1, n_wide)]
    cross = [send(theirs[n], n, 1) for n in range(n_wide)]
    chip_seqs = 2 * seq_dev
    scored = kernel(
        score_body,
        shaped(n_query, n_wide * chip_seqs),
        [pltpu.VMEM((share // 128, n_wide * chip_seqs * half, 128), FLOAT), pltpu.VMEM((n_query, n_wide * chip_seqs), FLOAT)],
        2 * n_query * n_wide * chip_seqs * half * share,
    )(in_specs=[SMEM] + [VMEM] * 9, out_specs=VMEM)(at, weighted, *same, *cross)
    return finish(scored, candidate, n_wide, n_layer, chip_seqs)


def solution(mesh):
    sizes = tuple(mesh.shape[a] for a in ("groups", "wide", "layer", "rep"))
    body = local_fast if sizes == (2, 4, 2, 2) else local
    in_specs = (
        P(("groups", "wide", "rep"), None, "layer"),
        P(("groups", "wide", "rep"), None, "layer"),
        P(("groups", "wide", "rep")),
        P("wide", "layer"),
        P("wide", "layer"),
        P(None, ("wide", "rep"), "layer"),
        P(("wide", "rep"), "layer"),
        P(("layer", "rep"), "groups"),
    )
    out_specs = P(("layer", "rep"), ("groups", "wide"))
    return jax.shard_map(body, mesh=mesh, in_specs=in_specs, out_specs=out_specs, check_vma=False)
```
